128 devices in a mesh: tm: 4 (over y_hi, core), height: 4 (over z), head: 8 (over x, y_lo).
Axes of the slice: x: 4, y: 4 (y_hi: 2, y_lo: 2; y = y_hi * 2 + y_lo), z: 4, core: 2. Of those that a mesh axis runs over, the one named last changes fastest.
Arguments:
- queries: bfloat16 [8, 4, 4, 4, 256, 128], P('head', 'tm', 'height'), may hold values from -8 to 8
- key_tiles: bfloat16 [8, 4, 4, 4, 256, 128], P('head', 'tm', 'height'), may hold values from -8 to 8
- values: bfloat16 [8, 4, 4, 4, 256, 128], P('head', 'tm', 'height'), may hold values from -6 to 6
- token_valid: int32 [4, 4, 4, 256], replicated, may hold values from 0 to 1, as said below
- out_weight: bfloat16 [1536, 1024], P(None, 'head'), may hold values from -2.5 to 2.5
- out_grad: bfloat16 [1536, 4, 4, 4, 256], P(None, 'tm', 'height'), may hold values from -2 to 2
Outputs:
- mixed: bfloat16 [1536, 4, 4, 4, 256], P('head', 'tm', 'height')
- query_grad: bfloat16 [8, 4, 4, 4, 256, 128], P('head', 'tm', 'height')
- key_grad: bfloat16 [8, 4, 4, 4, 256, 128], P('head', 'tm', 'height')
- value_grad: bfloat16 [8, 4, 4, 4, 256, 128], P('head', 'tm', 'height')
- weight_grad: float32 [1536, 1024], P(('tm', 'height'), 'head')
The draws below stay inside these ranges and needn't reach their ends.
Inputs may be any that keep to these rules, and one draw needn't show every extreme that they name: `token_valid`: A token is valid when its frame lies below the clip's frame extent, at least 13; its row below its frame's own row extent, from 25 to 31; and its column below its frame's and row's own column extent, from 25 to 31.
All inputs are finite; a program needn't handle non-finite values.
Results may differ from the reference program's by a relative error of at most 0.025.
Values may be sent and summed in bfloat16 or wider, within the bound.
A program may use at most 192 MiB of HBM per device.

```python
import math
import jax
import jax.numpy as jnp
from jax import lax

D = 1536
HD = 128
HEADS = 8
FT = 4
RT = 8
CT = 8
TILES_W = 4
TILE_TOK = 256
TILES_T = 4
TILES_H = 4
FRAMES = 16
ROWS = 32
COLS = 32


def planted_pattern(key):
    sign_key, level_key = jax.random.split(key)
    signs = jnp.where(jax.random.bernoulli(sign_key, 0.5, (HEADS, TILES_T, TILES_H, HD)), 1.0, -1.0)
    levels = jax.random.uniform(level_key, (HEADS, TILES_T, TILES_H), jnp.float32, 150.0, 300.0)
    amplitude = jnp.sqrt(levels) / HD ** 0.25
    planted = amplitude[:, :, :, None] * signs
    return (planted, levels)


def normal_values(key, factor):
    full_shape = (HEADS, TILES_T, TILES_H, TILES_W, TILE_TOK, HD)
    return jnp.clip(factor * jax.random.normal(key, full_shape, jnp.float32), -8.0, 8.0)


def draw_queries(key, part):
    planted, levels = planted_pattern(key)
    key = jax.random.fold_in(key, 3)
    base_values = normal_values(key, 1.4)
    return base_values.at[:, :, :, 0, 0, :].set(planted).astype(jnp.bfloat16)


def draw_key_tiles(key, part):
    planted, levels = planted_pattern(key)
    key = jax.random.fold_in(key, 5)
    base_values = normal_values(key, 1.4)
    base_values = base_values.at[:, :, :, 0, 0, :].set(planted)
    return base_values.at[:, :, :, 1, 0, :].set(planted * (1.0 - 2.0 / levels)[:, :, :, None]).astype(jnp.bfloat16)


def draw_token_valid(key, part):
    key = jax.random.fold_in(key, 7)
    frame_key, row_key, col_key = jax.random.split(key, 3)
    frame_extent = jax.random.randint(frame_key, (), FRAMES - FT + 1, FRAMES + 1)
    row_extent = jax.random.randint(row_key, (FRAMES,), ROWS - RT + 1, ROWS)
    col_extent = jax.random.randint(col_key, (FRAMES, ROWS), COLS - CT + 1, COLS)
    position = jnp.arange(TILE_TOK, dtype=jnp.int32)
    frame_of = jnp.arange(TILES_T, dtype=jnp.int32)[:, None] * FT + position[None, :] // (RT * CT)
    row_of = jnp.arange(TILES_H, dtype=jnp.int32)[:, None] * RT + position[None, :] // CT % RT
    col_of = jnp.arange(TILES_W, dtype=jnp.int32)[:, None] * CT + position[None, :] % CT
    frame_grid = jnp.broadcast_to(frame_of[:, None, None, :], (TILES_T, TILES_H, TILES_W, TILE_TOK))
    row_grid = jnp.broadcast_to(row_of[None, :, None, :], (TILES_T, TILES_H, TILES_W, TILE_TOK))
    col_grid = jnp.broadcast_to(col_of[None, None, :, :], (TILES_T, TILES_H, TILES_W, TILE_TOK))
    inside = (frame_grid < frame_extent) & (row_grid < row_extent[frame_grid]) & (col_grid < col_extent[frame_grid, row_grid])
    return inside.astype(jnp.int32)


def raised(entries, own_key, source, target, blocks, factor):
    def block_of(axis_at):
        return (jnp.arange(entries.shape[axis_at]) // (entries.shape[axis_at] // blocks)).reshape((-1,) + (1,) * (entries.ndim - 1 - axis_at))

    first = jax.random.permutation(own_key, blocks)[block_of(target)]
    second = (block_of(target) + blocks // 2) % blocks
    return jnp.where((block_of(source) == first) | (block_of(source) == second), factor * entries, entries)


def block_scale(stream_key, dims, shards, low, high):
    factor_of, own = 1.0, jax.random.fold_in(stream_key, 6)
    for dim, parts in shards:
        heights = jnp.exp(jax.random.uniform(jax.random.fold_in(own, dim), (parts,), jnp.float32, low / len(shards), high / len(shards)))
        factor_of = factor_of * jnp.repeat(heights, dims[dim] // parts).reshape([-1 if axis == dim else 1 for axis in range(len(dims))])
    return factor_of


def scatter_about(own_key, extent, spread, most, cuts=(), kind=jnp.bfloat16):
    result = jax.random.normal(own_key, extent, jnp.float32) * spread
    if len(cuts) > 0:
        result = block_scale(own_key, extent, cuts, -0.22, 0.18) * result
    return jnp.clip(result, min=-most, max=most).astype(kind)


def gaussian_with(own_key, dims, deviation, reach, cuts, heavy, kind=jnp.bfloat16):
    drawn = deviation * jax.random.normal(own_key, dims, jnp.float32)
    if cuts:
        drawn = drawn * block_scale(own_key, dims, cuts, -0.22, 0.18)
    return jnp.clip(raised(drawn, jax.random.fold_in(own_key, 3), *heavy), -reach, reach).astype(kind)


def setup_inputs(seed: int = 0) -> dict:
    streams_of = jax.random.split(jax.random.key(seed), 7)
    return {
        "queries": draw_queries(jax.random.fold_in(streams_of[6], 71), 0),
        "key_tiles": draw_key_tiles(jax.random.fold_in(streams_of[6], 71), 0),
        "values": scatter_about(streams_of[2], (HEADS, TILES_T, TILES_H, TILES_W, TILE_TOK, HD), 1.0, 6.0, ((0, 8), (1, 4), (2, 4))),
        "token_valid": draw_token_valid(jax.random.fold_in(streams_of[6], 71), 0),
        "out_weight": gaussian_with(streams_of[4], (D, HEADS * HD), 0.3, 2.5, ((1, 8),), (1, 0, 8, 2.0)),
        "out_grad": gaussian_with(streams_of[5], (D, TILES_T, TILES_H, TILES_W, TILE_TOK), 0.25, 2.0, ((1, 4), (2, 4)), (1, 0, 4, 2.0)),
    }


masked_score = -1e+30

def rounded(source):
    return lax.optimization_barrier(source.astype(jnp.bfloat16))

def pad_tiles(source, leading):
    margins = [(0, 0)] * leading + [(1, 1)] * 3 + [(0, 0)] * (source.ndim - leading - 3)
    return jnp.pad(source, margins)

def own_tile(source, leading, along_time, along_rows, along_cols):
    anchor = jnp.zeros((), jnp.int32)
    starts = [anchor] * leading + [along_time, along_rows, along_cols] + [anchor] * (source.ndim - leading - 3)
    extents = list(source.shape[:leading]) + [1, 1, 1] + list(source.shape[leading + 3:])
    picked = lax.dynamic_slice(source, starts, extents)
    return picked.reshape(tuple(source.shape[:leading]) + tuple(source.shape[leading + 3:]))

def tile_window(source, leading, along_time, along_rows, along_cols):
    anchor = jnp.zeros((), jnp.int32)
    starts = [anchor] * leading + [along_time, along_rows, along_cols] + [anchor] * (source.ndim - leading - 3)
    extents = list(source.shape[:leading]) + [3, 3, 3] + list(source.shape[leading + 3:])
    window_block = lax.dynamic_slice(source, starts, extents)
    merged_shape = tuple(source.shape[:leading]) + (27 * source.shape[leading + 3],) + tuple(source.shape[leading + 4:])
    return window_block.reshape(merged_shape)

def untile(stacked):
    moved = jnp.moveaxis(stacked, 0, 1)
    return moved.reshape((moved.shape[0], TILES_T, TILES_H, TILES_W) + tuple(moved.shape[2:]))

def reference(queries, key_tiles, values, token_valid, out_weight, out_grad):
    factor = 1.0 / math.sqrt(HD)
    flat_ids = jnp.arange(TILES_T * TILES_H * TILES_W, dtype=jnp.int32)
    key_pad = pad_tiles(key_tiles, 1)
    value_pad = pad_tiles(values, 1)
    valid_pad = pad_tiles(token_valid, 0)

    def locate(flat_index):
        along_time = flat_index // (TILES_H * TILES_W)
        along_rows = flat_index // TILES_W % TILES_H
        along_cols = flat_index % TILES_W
        return (along_time, along_rows, along_cols)

    def forward_tile(flat_index):
        along_time, along_rows, along_cols = locate(flat_index)
        query_now = own_tile(queries, 1, along_time, along_rows, along_cols).astype(jnp.float32)
        key_near = tile_window(key_pad, 1, along_time, along_rows, along_cols).astype(jnp.float32)
        value_near = tile_window(value_pad, 1, along_time, along_rows, along_cols).astype(jnp.float32)
        near_ok = tile_window(valid_pad, 0, along_time, along_rows, along_cols) > 0
        scores = jnp.einsum('hne,hme->hnm', query_now, key_near) * factor
        scores = jnp.where(near_ok, scores, masked_score)
        highest = lax.optimization_barrier(jnp.max(scores, axis=-1, keepdims=True))
        grand_total = lax.optimization_barrier(jnp.sum(jnp.where(near_ok, jnp.exp(scores - highest), 0.0), axis=-1, keepdims=True))
        log_total = highest + jnp.log(grand_total)
        weights = rounded(jnp.where(near_ok, jnp.exp(scores - log_total), 0.0)).astype(jnp.float32)
        attended = jnp.einsum('hnm,hme->hne', weights, value_near).astype(jnp.bfloat16)
        return (attended, log_total[..., 0])
    attended_tiles, total_tiles = lax.map(forward_tile, flat_ids)
    attended = untile(attended_tiles)
    log_sum = untile(total_tiles)
    attended_wide = lax.optimization_barrier(attended).astype(jnp.float32)
    weight_heads = out_weight.reshape(D, HEADS, HD).astype(jnp.float32)
    mixed = jnp.einsum('dhe,habcne->dabcn', weight_heads, attended_wide).astype(jnp.bfloat16)
    grad_wide = out_grad.astype(jnp.float32)
    grad_attended = rounded(jnp.einsum('dabcn,dhe->habcne', grad_wide, weight_heads))
    row_delta = lax.optimization_barrier(jnp.sum(grad_attended.astype(jnp.float32) * attended_wide, axis=-1))
    weight_grad = jnp.einsum('dabcn,habcne->dhe', grad_wide, attended_wide).reshape(D, HEADS * HD)

    def query_tile(flat_index):
        along_time, along_rows, along_cols = locate(flat_index)
        query_now = own_tile(queries, 1, along_time, along_rows, along_cols).astype(jnp.float32)
        grad_now = own_tile(grad_attended, 1, along_time, along_rows, along_cols).astype(jnp.float32)
        total_now = own_tile(log_sum, 1, along_time, along_rows, along_cols)
        delta_now = own_tile(row_delta, 1, along_time, along_rows, along_cols)
        key_near = tile_window(key_pad, 1, along_time, along_rows, along_cols).astype(jnp.float32)
        value_near = tile_window(value_pad, 1, along_time, along_rows, along_cols).astype(jnp.float32)
        near_ok = tile_window(valid_pad, 0, along_time, along_rows, along_cols) > 0
        scores = jnp.einsum('hne,hme->hnm', query_now, key_near) * factor
        probs = jnp.where(near_ok, jnp.exp(jnp.where(near_ok, scores, masked_score) - total_now[..., None]), 0.0)
        grad_probs = jnp.einsum('hne,hme->hnm', grad_now, value_near)
        grad_scores = rounded(probs * (grad_probs - delta_now[..., None])).astype(jnp.float32)
        return (jnp.einsum('hnm,hme->hne', grad_scores, key_near) * factor).astype(jnp.bfloat16)
    query_grad = untile(lax.map(query_tile, flat_ids))
    query_pad = pad_tiles(queries, 1)
    grad_pad = pad_tiles(grad_attended, 1)
    total_pad = pad_tiles(log_sum, 1)
    delta_pad = pad_tiles(row_delta, 1)
    inside_pad = pad_tiles(jnp.ones((TILES_T, TILES_H, TILES_W, TILE_TOK), jnp.int32), 0)

    def key_tile(flat_index):
        along_time, along_rows, along_cols = locate(flat_index)
        query_near = tile_window(query_pad, 1, along_time, along_rows, along_cols).astype(jnp.float32)
        grad_near = tile_window(grad_pad, 1, along_time, along_rows, along_cols).astype(jnp.float32)
        total_near = tile_window(total_pad, 1, along_time, along_rows, along_cols)
        delta_near = tile_window(delta_pad, 1, along_time, along_rows, along_cols)
        inside_near = tile_window(inside_pad, 0, along_time, along_rows, along_cols) > 0
        key_now = own_tile(key_tiles, 1, along_time, along_rows, along_cols).astype(jnp.float32)
        value_now = own_tile(values, 1, along_time, along_rows, along_cols).astype(jnp.float32)
        key_ok = own_tile(token_valid, 0, along_time, along_rows, along_cols) > 0
        pair_ok = jnp.logical_and(inside_near[:, None], key_ok[None, :])
        scores = jnp.einsum('hqe,hke->hqk', query_near, key_now) * factor
        probs = jnp.where(pair_ok, jnp.exp(jnp.where(pair_ok, scores, masked_score) - total_near[..., None]), 0.0)
        weights = rounded(probs).astype(jnp.float32)
        value_part = jnp.einsum('hqk,hqe->hke', weights, grad_near)
        grad_probs = jnp.einsum('hqe,hke->hqk', grad_near, value_now)
        grad_scores = rounded(probs * (grad_probs - delta_near[..., None])).astype(jnp.float32)
        key_part = jnp.einsum('hqk,hqe->hke', grad_scores, query_near) * factor
        return (key_part.astype(jnp.bfloat16), value_part.astype(jnp.bfloat16))
    key_parts, value_parts = lax.map(key_tile, flat_ids)
    key_grad = untile(key_parts)
    value_grad = untile(value_parts)
    return (mixed, query_grad, key_grad, value_grad, weight_grad)
```

```python
import functools
import math

import jax
import jax.numpy as jnp
from jax import lax
from jax.experimental import pallas as pl
from jax.experimental.pallas import tpu as pltpu
from jax.sharding import PartitionSpec as P

MESH = pl.DeviceIdType.MESH
F32 = jnp.float32
BF16 = jnp.bfloat16

TILE = 256
SPAN = 4
TOKENS = TILE * SPAN
HD = 128
D = 1536
HEADS = 8
NT = 4
NH = 4
GROUP = NT * NH
SCALE = 1.0 / math.sqrt(HD)
EXPO = SCALE * math.log2(math.e)
LOWEST = -1e30

SLOTS = 9
BACK_ORDER = (7, 8, 5, 6, 3, 4, 2, 1, 0)

PAIRS = [(k, q) for k in range(SPAN) for q in range(SPAN) if abs(k - q) <= 1]
PAIR_AT = {pair: i for i, pair in enumerate(PAIRS)}


def dot(lhs, rhs, dims=((1,), (0,))):
    return lax.dot_general(lhs, rhs, (dims, ((), ())), preferred_element_type=F32)


def chosen(index, table):
    value = jnp.int32(table[0])
    for at, entry in enumerate(table):
        value = jnp.where(index == at, jnp.int32(entry), value)
    return value


def kernel(
    q_ref, k_ref, v_ref, tv_ref, w_ref, og_ref,
    mixed_ref, dq_ref, dk_ref, dv_ref, wg_ref,
    q_s, kv_s, kt_s, vt_s, mask_s, w_s, og_s,
    qt_s, do_s, dot_s, p_s, ps_s, ds_s, att_s, m_s, mb_s, rl_s, dqt_s,
    acc_s, send_s, rp_s, rz_s, rx_s, ry_s, ag_s, wgat_s, prod_s, red_s,
    loc_sem, f_send, f_recv, b_send, b_recv, ag_send, ag_recv, wt_send, wt_recv, pr_send, pr_recv,
):
    a = lax.axis_index("tm")
    b = lax.axis_index("height")
    h = lax.axis_index("head")
    inner = jnp.logical_or(a == 1, a == 2)
    has_lo = b > 0
    has_hi = b < NH - 1
    partner = a + 1 - 2 * (a % 2)
    cross = NT - 1 - a
    here = a * NH + b
    dev_partner = (partner, b, h)
    dev_cross = (cross, b, h)
    dev_lo = (a, b - 1, h)
    dev_hi = (a, b + 1, h)
    both = jnp.logical_and

    loads = [
        pltpu.make_async_copy(src, dst, loc_sem.at[i])
        for i, (src, dst) in enumerate(
            [(q_ref, q_s), (k_ref, kv_s.at[0, 0]), (v_ref, kv_s.at[0, 1]), (w_ref, w_s), (og_ref, og_s)]
        )
    ]
    for load in loads:
        load.start()

    barrier = pltpu.get_barrier_semaphore()
    for j in range(1, GROUP):
        peer = (here + j) % GROUP
        pl.semaphore_signal(barrier, inc=1, device_id=(peer // NH, peer % NH, h), device_id_type=MESH)
    for j in range(1, HEADS):
        pl.semaphore_signal(barrier, inc=1, device_id=(a, b, (h + j) % HEADS), device_id_type=MESH)
    pl.semaphore_wait(barrier, GROUP - 1 + HEADS - 1)

    def remote(src, dst, send, recv, device):
        return pltpu.make_async_remote_copy(
            src_ref=src, dst_ref=dst, send_sem=send, recv_sem=recv, device_id=device, device_id_type=MESH
        )

    yes = a >= 0
    hops = [
        (-1, 3, dev_hi, has_hi),
        (-1, 4, dev_lo, has_lo),
        (-1, 2, dev_cross, inner),
        (-1, 1, dev_partner, yes),
        (3, 5, dev_partner, has_lo),
        (4, 6, dev_partner, has_hi),
        (2, 7, dev_hi, both(inner, has_hi)),
        (2, 8, dev_lo, both(inner, has_lo)),
    ]
    arrives = [yes, yes, inner, has_lo, has_hi, has_lo, has_hi, both(inner, has_lo), both(inner, has_hi)]

    def hop_copies(n):
        source, target, device, _ = hops[n]
        return [
            remote(
                (k_ref, v_ref)[i] if source < 0 else kv_s.at[source, i],
                kv_s.at[target, i], f_send.at[n, i], f_recv.at[target, i], device,
            )
            for i in range(2)
        ]

    def start_hop(n):
        @pl.when(hops[n][3])
        def _():
            for copy in hop_copies(n):
                copy.start()

    def wait_slot(slot):
        @pl.when(arrives[slot])
        def _():
            for i in range(2):
                remote(
                    k_ref, kv_s.at[slot, i], f_send.at[0, 0], f_recv.at[slot, i], dev_partner
                ).wait_recv()

    for n in range(4):
        start_hop(n)

    share = D // HEADS

    def weight_copy(j):
        peer = (h + j) % HEADS
        return remote(
            w_ref.at[pl.ds(pl.multiple_of(peer * share, share), share)], wgat_s.at[h],
            wt_send.at[j], wt_recv.at[j], (a, b, peer),
        )

    for j in range(1, HEADS):
        weight_copy(j).start()

    for load in loads[:3]:
        load.wait()
    first_row = (lax.broadcasted_iota(jnp.int32, (HD, TILE), 0) == 0).astype(BF16)
    for c in range(SPAN):
        rows = slice(c * TILE, (c + 1) * TILE)
        qt_s[c, :HD] = q_s[rows].T
        qt_s[c, HD:] = first_row
        m_s[c] = jnp.full((1, TILE), LOWEST, F32)
        att_s[c] = jnp.zeros((HD + 16, TILE), F32)
    ones_rows = jnp.ones((16, TOKENS), BF16)
    ones_cols = jnp.ones((TILE, HD), BF16)

    def span_of(c):
        return max(0, c - 1), min(SPAN, c + 2)

    def place(slot):
        frame = chosen(slot, (0, 1, 2, 0, 0, 1, 1, 2, 2))
        frame = jnp.where(frame == 0, a, jnp.where(frame == 1, partner, cross))
        row = b + chosen(slot, (0, 0, 0, -1, 1, -1, 1, -1, 1))
        return frame, row

    def exists(slot):
        far = chosen(slot, (0, 0, 1, 0, 0, 0, 0, 1, 1))
        row = b + chosen(slot, (0, 0, 0, -1, 1, -1, 1, -1, 1))
        near = both(row >= 0, row < NH)
        return both(near, jnp.logical_or(far == 0, inner))

    def forward_column(slot):
        frame, row = place(slot)
        for c in range(SPAN):
            rows = slice(c * TILE, (c + 1) * TILE)
            kt_s[slot, :, rows] = kv_s[slot, 0, rows].T
            vt_s[slot, :, rows] = kv_s[slot, 1, rows].T
            valid = tv_ref[pl.ds((frame * NH + row) * SPAN + c, 1), :]
            bias = jnp.where(valid > 0, 0.0, LOWEST)
            mask_s[rows] = jnp.broadcast_to(bias, (HD, TILE)).T.astype(BF16)
        for c in range(SPAN):
            lo, hi = span_of(c)
            rows = slice(lo * TILE, hi * TILE)
            keys = jnp.concatenate([kv_s[slot, 0, rows], mask_s[rows]], axis=1)
            scores = dot(keys, qt_s[c])
            old = m_s[c]
            new = jnp.maximum(old, jnp.max(scores, axis=0, keepdims=True))
            weights = jnp.exp2((scores - new) * EXPO).astype(BF16)
            for t in range(lo, hi):
                p_s[slot, PAIR_AT[t, c]] = weights[(t - lo) * TILE:(t - lo + 1) * TILE]
            vals = jnp.concatenate([vt_s[slot, :, rows], ones_rows[:, rows]], axis=0)
            att_s[c] = att_s[c] * jnp.exp2((old - new) * EXPO) + dot(vals, weights)
            m_s[c] = new
            mb_s[slot, c] = new

    def grad_attended():
        for load in loads[3:]:
            load.wait()
        for c in range(SPAN):
            rows = slice(c * TILE, (c + 1) * TILE)
            grad = dot(w_s[...], og_s[:, rows], ((0,), (0,))).astype(BF16)
            dot_s[c, :HD] = grad
            do_s[rows] = grad.T

    def forward_step(i, carry):
        @pl.when(i == 1)
        def _():
            grad_attended()
            wait_slot(1)

        @pl.when(i == 2)
        def _():
            wait_slot(2)
            start_hop(6)
            start_hop(7)

        @pl.when(i == 3)
        def _():
            wait_slot(3)
            start_hop(4)
            wait_slot(4)
            start_hop(5)

        for slot in range(5, SLOTS):
            @pl.when(i == slot)
            def _():
                wait_slot(slot)

        @pl.when(exists(i))
        def _():
            forward_column(i)

        return carry

    lax.fori_loop(0, SLOTS, forward_step, 0)

    for c in range(SPAN):
        rows = slice(c * TILE, (c + 1) * TILE)
        inverse = 1.0 / att_s[c, HD:HD + 1]
        rl_s[c] = inverse
        attended = (att_s[c, :HD] * inverse).astype(BF16)
        ag_s[h, :, rows] = attended
        delta = jnp.sum(dot_s[c, :HD].astype(F32) * attended.astype(F32), axis=0, keepdims=True)
        high = delta.astype(BF16).astype(F32)
        middle = (delta - high).astype(BF16).astype(F32)
        low = delta - high - middle
        index = lax.broadcasted_iota(jnp.int32, (HD, TILE), 0)
        extra = jnp.where(index == 0, -high, jnp.where(index == 1, -middle, jnp.where(index == 2, -low, 0.0)))
        dot_s[c, HD:] = extra.astype(BF16)
        dqt_s[c] = jnp.zeros((HD, TILE), F32)

    def gather_copy(j):
        return remote(ag_s.at[h], ag_s.at[h], ag_send.at[j], ag_recv.at[j], (a, b, (h + j) % HEADS))

    for j in range(1, HEADS):
        gather_copy(j).start()

    part = D // GROUP

    def part_copy(j):
        peer = (here + j) % GROUP
        return remote(
            prod_s.at[peer], red_s.at[here], pr_send.at[j], pr_recv.at[j], (peer // NH, peer % NH, h)
        )

    for n in range(GROUP):
        prod_s[n] = dot(og_s[n * part:(n + 1) * part], ag_s[h], ((1,), (1,))).astype(BF16)
    for j in range(1, GROUP):
        part_copy(j).start()

    def backward_column(slot):
        factors = [
            jnp.exp2((mb_s[slot, c] - m_s[c]) * EXPO) * rl_s[c] for c in range(SPAN)
        ]
        for t in range(SPAN):
            rows = slice(t * TILE, (t + 1) * TILE)
            lo, hi = span_of(t)
            vals = jnp.concatenate([kv_s[slot, 1, rows], ones_cols], axis=1)
            for c in range(lo, hi):
                n = PAIR_AT[t, c]
                grad = dot(vals, dot_s[c])
                probs = p_s[slot, n].astype(F32) * factors[c]
                ps_s[n] = probs.astype(BF16)
                ds_s[n] = (probs * grad).astype(BF16)
            near = slice(lo * TILE, hi * TILE)
            many_ds = jnp.concatenate([ds_s[PAIR_AT[t, c]] for c in range(lo, hi)], axis=1)
            many_ps = jnp.concatenate([ps_s[PAIR_AT[t, c]] for c in range(lo, hi)], axis=1)
            acc_s[0, rows] = dot(many_ds, q_s[near]) * SCALE
            acc_s[1, rows] = dot(many_ps, do_s[near])
        for c in range(SPAN):
            lo, hi = span_of(c)
            many = jnp.concatenate([ds_s[PAIR_AT[t, c]] for t in range(lo, hi)], axis=0)
            dqt_s[c] += dot(kt_s[slot, :, lo * TILE:hi * TILE], many)

    back = {
        7: (rx_s.at[0], 0, dev_lo, both(inner, has_lo)),
        8: (rx_s.at[1], 1, dev_hi, both(inner, has_hi)),
        5: (rp_s.at[1], 2, dev_partner, has_lo),
        6: (rp_s.at[2], 3, dev_partner, has_hi),
        3: (rz_s.at[0], 4, dev_lo, has_lo),
        4: (rz_s.at[1], 5, dev_hi, has_hi),
        2: (ry_s, 6, dev_cross, inner),
        1: (rp_s.at[0], 7, dev_partner, yes),
    }
    back_arrives = {
        7: both(inner, has_hi), 8: both(inner, has_lo), 5: has_lo, 6: has_hi,
        3: has_hi, 4: has_lo, 2: inner, 1: yes,
    }

    def back_copy(slot):
        target, index, device, _ = back[slot]
        return remote(send_s.at[slot - 1], target, b_send.at[slot - 1], b_recv.at[index], device)

    def add_arrived(slot):
        @pl.when(back_arrives[slot])
        def _():
            back_copy(slot).wait_recv()
            acc_s[...] += back[slot][0][...].astype(F32)

    needs = {7: (), 8: (), 5: (), 6: (), 3: (5,), 4: (6,), 2: (7, 8), 1: ()}

    def backward_step(i, carry):
        slot = chosen(i, BACK_ORDER)

        @pl.when(exists(slot))
        def _():
            backward_column(slot)

        for n in range(1, SLOTS):
            @pl.when(both(slot == n, back[n][3]))
            def _():
                for source in needs[n]:
                    add_arrived(source)
                send_s[n - 1] = acc_s[...].astype(BF16)
                back_copy(n).start()

        return carry

    lax.fori_loop(0, SLOTS, backward_step, 0)

    for c in range(SPAN):
        rows = slice(c * TILE, (c + 1) * TILE)
        dq_ref[rows] = (dqt_s[c] * SCALE).T.astype(BF16)

    loads_w = w_s[pl.ds(pl.multiple_of(h * share, share), share)]
    wgat_s[h] = loads_w
    for j in range(1, HEADS):
        weight_copy(j).wait_recv()
        gather_copy(j).wait_recv()
    weights = jnp.concatenate([wgat_s[n] for n in range(HEADS)], axis=1)
    for c in range(SPAN):
        rows = slice(c * TILE, (c + 1) * TILE)
        everyone = jnp.concatenate([ag_s[n, :, rows] for n in range(HEADS)], axis=0)
        mixed_ref[:, rows] = dot(weights, everyone).astype(BF16)

    red_s[here] = prod_s[here]
    for j in range(1, GROUP):
        part_copy(j).wait_recv()
    total = red_s[0].astype(F32)
    for n in range(1, GROUP):
        total = total + red_s[n].astype(F32)
    wg_ref[...] = total

    for slot in (1, 4, 3, 2):
        add_arrived(slot)
    dk_ref[...] = acc_s[0].astype(BF16)
    dv_ref[...] = acc_s[1].astype(BF16)

    for n in range(len(hops)):
        @pl.when(hops[n][3])
        def _():
            for copy in hop_copies(n):
                copy.wait_send()
    for slot in range(1, SLOTS):
        @pl.when(back[slot][3])
        def _():
            back_copy(slot).wait_send()
    for j in range(1, HEADS):
        weight_copy(j).wait_send()
        gather_copy(j).wait_send()
    for j in range(1, GROUP):
        part_copy(j).wait_send()


def per_device(queries, key_tiles, values, token_valid, out_weight, out_grad):
    any_spec = pl.BlockSpec(memory_space=pl.ANY)
    vmem_spec = pl.BlockSpec(memory_space=pltpu.VMEM)
    vmem = pltpu.VMEM
    dma = pltpu.SemaphoreType.DMA
    token = jax.ShapeDtypeStruct((TOKENS, HD), BF16)
    pair = (2, TOKENS, HD)
    mixed, dq, dk, dv, wg = pl.pallas_call(
        kernel,
        out_shape=(
            jax.ShapeDtypeStruct((D // HEADS, TOKENS), BF16),
            token, token, token,
            jax.ShapeDtypeStruct((D // GROUP, HD), F32),
        ),
        in_specs=[any_spec, any_spec, any_spec, vmem_spec, any_spec, any_spec],
        out_specs=(vmem_spec,) * 5,
        scratch_shapes=[
            vmem((TOKENS, HD), BF16),
            vmem((SLOTS,) + pair, BF16),
            vmem((SLOTS, HD, TOKENS), BF16),
            vmem((SLOTS, HD, TOKENS), BF16),
            vmem((TOKENS, HD), BF16),
            vmem((D, HD), BF16),
            vmem((D, TOKENS), BF16),
            vmem((SPAN, 2 * HD, TILE), BF16),
            vmem((TOKENS, HD), BF16),
            vmem((SPAN, 2 * HD, TILE), BF16),
            vmem((SLOTS, len(PAIRS), TILE, TILE), BF16),
            vmem((len(PAIRS), TILE, TILE), BF16),
            vmem((len(PAIRS), TILE, TILE), BF16),
            vmem((SPAN, HD + 16, TILE), F32),
            vmem((SPAN, 1, TILE), F32),
            vmem((SLOTS, SPAN, 1, TILE), F32),
            vmem((SPAN, 1, TILE), F32),
            vmem((SPAN, HD, TILE), F32),
            vmem(pair, F32),
            vmem((SLOTS - 1,) + pair, BF16),
            vmem((3,) + pair, BF16),
            vmem((2,) + pair, BF16),
            vmem((2,) + pair, BF16),
            vmem(pair, BF16),
            vmem((HEADS, HD, TOKENS), BF16),
            vmem((HEADS, D // HEADS, HD), BF16),
            vmem((GROUP, D // GROUP, HD), BF16),
            vmem((GROUP, D // GROUP, HD), BF16),
            dma((5,)), dma((8, 2)), dma((SLOTS, 2)), dma((SLOTS - 1,)), dma((SLOTS - 1,)),
            dma((HEADS,)), dma((HEADS,)), dma((HEADS,)), dma((HEADS,)), dma((GROUP,)), dma((GROUP,)),
        ],
        compiler_params=pltpu.CompilerParams(
            collective_id=0, has_side_effects=True, vmem_limit_bytes=60 * 1024 * 1024
        ),
    )(
        queries.reshape(TOKENS, HD),
        key_tiles.reshape(TOKENS, HD),
        values.reshape(TOKENS, HD),
        token_valid.reshape(GROUP * SPAN, TILE),
        out_weight,
        out_grad.reshape(D, TOKENS),
    )
    tile_shape = (1, 1, 1, SPAN, TILE, HD)
    return (
        mixed.reshape(D // HEADS, 1, 1, SPAN, TILE),
        dq.reshape(tile_shape),
        dk.reshape(tile_shape),
        dv.reshape(tile_shape),
        wg,
    )


def solution(mesh):
    placed = (
        P("head", "tm", "height", None, None, None),
        P("head", "tm", "height", None, None, None),
        P("head", "tm", "height", None, None, None),
        P(),
        P(None, "head"),
        P(None, "tm", "height", None, None),
    )
    return jax.shard_map(
        per_device,
        mesh=mesh,
        in_specs=placed,
        out_specs=(
            P("head", "tm", "height", None, None),
            P("head", "tm", "height", None, None, None),
            P("head", "tm", "height", None, None, None),
            P("head", "tm", "height", None, None, None),
            P(("tm", "height"), "head"),
        ),
        check_vma=False,
    )
```

```python
import functools
import math

import jax
import jax.numpy as jnp
from jax import lax
from jax.experimental import pallas as pl
from jax.experimental.pallas import tpu as pltpu
from jax.sharding import PartitionSpec as P

MESH = pl.DeviceIdType.MESH
F32 = jnp.float32
BF16 = jnp.bfloat16

TILE = 256
SPAN = 4
TOKENS = TILE * SPAN
HD = 128
D = 1536
HEADS = 8
NT = 4
NH = 4
GROUP = NT * NH
SCALE = 1.0 / math.sqrt(HD)
EXPO = SCALE * math.log2(math.e)
LOWEST = -1e30

SLOTS = 9
BACK_ORDER = (7, 8, 5, 6, 3, 4, 2, 1, 0)

PAIRS = [(k, q) for k in range(SPAN) for q in range(SPAN) if abs(k - q) <= 1]
PAIR_AT = {pair: i for i, pair in enumerate(PAIRS)}


def dot(lhs, rhs, dims=((1,), (0,))):
    return lax.dot_general(lhs, rhs, (dims, ((), ())), preferred_element_type=F32)


def chosen(index, table):
    value = jnp.int32(table[0])
    for at, entry in enumerate(table):
        value = jnp.where(index == at, jnp.int32(entry), value)
    return value


def kernel(
    q_ref, k_ref, v_ref, tv_ref, w_ref, og_ref,
    mixed_ref, dq_ref, dk_ref, dv_ref, wg_ref,
    q_s, kv_s, kt_s, vt_s, mask_s, w_s, raw_s, og_s,
    qt_s, do_s, dot_s, p_s, ps_s, ds_s, att_s, m_s, mb_s, rl_s, dqt_s,
    acc_s, send_s, rp_s, rz_s, rx_s, ry_s, ag_s, wgat_s, prod_s, red_s,
    loc_sem, f_send, f_recv, b_send, b_recv, ag_send, ag_recv, wt_send, wt_recv, pr_send, pr_recv,
):
    a = lax.axis_index("tm")
    b = lax.axis_index("height")
    h = lax.axis_index("head")
    inner = jnp.logical_or(a == 1, a == 2)
    has_lo = b > 0
    has_hi = b < NH - 1
    partner = a + 1 - 2 * (a % 2)
    cross = NT - 1 - a
    here = a * NH + b
    dev_partner = (partner, b, h)
    dev_cross = (cross, b, h)
    dev_lo = (a, b - 1, h)
    dev_hi = (a, b + 1, h)
    both = jnp.logical_and

    loads = [
        pltpu.make_async_copy(src, dst, loc_sem.at[i])
        for i, (src, dst) in enumerate(
            [(q_ref, q_s), (k_ref, kv_s.at[0, 0]), (v_ref, kv_s.at[0, 1]), (w_ref, w_s), (og_ref, raw_s)]
        )
    ]
    for load in loads:
        load.start()

    barrier = pltpu.get_barrier_semaphore()
    for j in range(1, GROUP):
        peer = (here + j) % GROUP
        pl.semaphore_signal(barrier, inc=1, device_id=(peer // NH, peer % NH, h), device_id_type=MESH)
    for j in range(1, HEADS):
        pl.semaphore_signal(barrier, inc=1, device_id=(a, b, (h + j) % HEADS), device_id_type=MESH)
    pl.semaphore_wait(barrier, GROUP - 1 + HEADS - 1)

    def remote(src, dst, send, recv, device):
        return pltpu.make_async_remote_copy(
            src_ref=src, dst_ref=dst, send_sem=send, recv_sem=recv, device_id=device, device_id_type=MESH
        )

    yes = a >= 0
    hops = [
        (-1, 3, dev_hi, has_hi),
        (-1, 4, dev_lo, has_lo),
        (-1, 2, dev_cross, inner),
        (-1, 1, dev_partner, yes),
        (3, 5, dev_partner, has_lo),
        (4, 6, dev_partner, has_hi),
        (2, 7, dev_hi, both(inner, has_hi)),
        (2, 8, dev_lo, both(inner, has_lo)),
    ]
    arrives = [yes, yes, inner, has_lo, has_hi, has_lo, has_hi, both(inner, has_lo), both(inner, has_hi)]

    def hop_copies(n):
        source, target, device, _ = hops[n]
        return [
            remote(
                (k_ref, v_ref)[i] if source < 0 else kv_s.at[source, i],
                kv_s.at[target, i], f_send.at[n, i], f_recv.at[target, i], device,
            )
            for i in range(2)
        ]

    def start_hop(n):
        @pl.when(hops[n][3])
        def _():
            for copy in hop_copies(n):
                copy.start()

    def wait_slot(slot):
        @pl.when(arrives[slot])
        def _():
            for i in range(2):
                remote(
                    k_ref, kv_s.at[slot, i], f_send.at[0, 0], f_recv.at[slot, i], dev_partner
                ).wait_recv()

    for n in range(4):
        start_hop(n)

    share = D // HEADS

    def weight_copy(j):
        peer = (h + j) % HEADS
        return remote(
            w_ref.at[pl.ds(pl.multiple_of(peer * share, share), share)], wgat_s.at[h],
            wt_send.at[j], wt_recv.at[j], (a, b, peer),
        )

    for j in range(1, HEADS):
        weight_copy(j).start()

    for load in loads[:3]:
        load.wait()
    first_row = (lax.broadcasted_iota(jnp.int32, (HD, TILE), 0) == 0).astype(BF16)
    for c in range(SPAN):
        rows = slice(c * TILE, (c + 1) * TILE)
        qt_s[c, :HD] = q_s[rows].T
        qt_s[c, HD:] = first_row
        m_s[c] = jnp.full((1, TILE), LOWEST, F32)
        att_s[c] = jnp.zeros((HD + 16, TILE), F32)
    ones_rows = jnp.ones((16, TOKENS), BF16)
    ones_cols = jnp.ones((TILE, HD), BF16)

    def span_of(c):
        return max(0, c - 1), min(SPAN, c + 2)

    def place(slot):
        frame = chosen(slot, (0, 1, 2, 0, 0, 1, 1, 2, 2))
        frame = jnp.where(frame == 0, a, jnp.where(frame == 1, partner, cross))
        row = b + chosen(slot, (0, 0, 0, -1, 1, -1, 1, -1, 1))
        return frame, row

    def exists(slot):
        far = chosen(slot, (0, 0, 1, 0, 0, 0, 0, 1, 1))
        row = b + chosen(slot, (0, 0, 0, -1, 1, -1, 1, -1, 1))
        near = both(row >= 0, row < NH)
        return both(near, jnp.logical_or(far == 0, inner))

    def forward_column(slot):
        frame, row = place(slot)
        for c in range(SPAN):
            rows = slice(c * TILE, (c + 1) * TILE)
            kt_s[slot, :, rows] = kv_s[slot, 0, rows].T
            vt_s[slot, :, rows] = kv_s[slot, 1, rows].T
            valid = tv_ref[frame, row, c:c + 1, :]
            bias = jnp.where(valid > 0, 0.0, LOWEST)
            mask_s[rows] = jnp.broadcast_to(bias, (HD, TILE)).T.astype(BF16)
        for c in range(SPAN):
            lo, hi = span_of(c)
            rows = slice(lo * TILE, hi * TILE)
            keys = jnp.concatenate([kv_s[slot, 0, rows], mask_s[rows]], axis=1)
            scores = dot(keys, qt_s[c])
            old = m_s[c]
            new = jnp.maximum(old, jnp.max(scores, axis=0, keepdims=True))
            weights = jnp.exp2((scores - new) * EXPO).astype(BF16)
            for t in range(lo, hi):
                p_s[slot, PAIR_AT[t, c]] = weights[(t - lo) * TILE:(t - lo + 1) * TILE]
            vals = jnp.concatenate([vt_s[slot, :, rows], ones_rows[:, rows]], axis=0)
            att_s[c] = att_s[c] * jnp.exp2((old - new) * EXPO) + dot(vals, weights)
            m_s[c] = new
            mb_s[slot, c] = new

    def grad_attended():
        for load in loads[3:]:
            load.wait()
        for n in range(0, D, HD):
            og_s[n:n + HD] = raw_s[n:n + HD].reshape(HD, TOKENS)
        for c in range(SPAN):
            rows = slice(c * TILE, (c + 1) * TILE)
            grad = dot(w_s[...], og_s[:, rows], ((0,), (0,))).astype(BF16)
            dot_s[c, :HD] = grad
            do_s[rows] = grad.T

    def forward_step(i, carry):
        @pl.when(i == 1)
        def _():
            grad_attended()
            wait_slot(1)

        @pl.when(i == 2)
        def _():
            wait_slot(2)
            start_hop(6)
            start_hop(7)

        @pl.when(i == 3)
        def _():
            wait_slot(3)
            start_hop(4)
            wait_slot(4)
            start_hop(5)

        for slot in range(5, SLOTS):
            @pl.when(i == slot)
            def _():
                wait_slot(slot)

        @pl.when(exists(i))
        def _():
            forward_column(i)

        return carry

    lax.fori_loop(0, SLOTS, forward_step, 0)

    for c in range(SPAN):
        rows = slice(c * TILE, (c + 1) * TILE)
        inverse = 1.0 / att_s[c, HD:HD + 1]
        rl_s[c] = inverse
        attended = (att_s[c, :HD] * inverse).astype(BF16)
        ag_s[h, :, rows] = attended
        delta = jnp.sum(dot_s[c, :HD].astype(F32) * attended.astype(F32), axis=0, keepdims=True)
        high = delta.astype(BF16).astype(F32)
        middle = (delta - high).astype(BF16).astype(F32)
        low = delta - high - middle
        index = lax.broadcasted_iota(jnp.int32, (HD, TILE), 0)
        extra = jnp.where(index == 0, -high, jnp.where(index == 1, -middle, jnp.where(index == 2, -low, 0.0)))
        dot_s[c, HD:] = extra.astype(BF16)
        dqt_s[c] = jnp.zeros((HD, TILE), F32)

    side = h + 1 - 2 * (h % 2)
    up, down = (h + 2) % HEADS, (h + HEADS - 2) % HEADS
    side_up, side_down = (side + 2) % HEADS, (side + HEADS - 2) % HEADS
    half = HD // 2
    low_half, high_half = pl.ds(0, half), pl.ds(half, half)
    gathers = [
        (ag_s.at[h], side),
        (ag_s.at[h], up),
        (ag_s.at[h], down),
        (ag_s.at[side], up),
        (ag_s.at[side], down),
        (ag_s.at[down, low_half], up),
        (ag_s.at[up, high_half], down),
        (ag_s.at[side_down, low_half], up),
        (ag_s.at[side_up, high_half], down),
    ]

    def gather_copy(n):
        block, peer = gathers[n]
        return remote(block, block, ag_send.at[n], ag_recv.at[n], (a, b, peer))

    def relay(waits, starts):
        for n in waits:
            gather_copy(n).wait_recv()
        for n in starts:
            gather_copy(n).start()

    relay((), (0, 1, 2))

    part = D // GROUP

    def part_copy(j):
        peer = (here + j) % GROUP
        return remote(
            prod_s.at[peer], red_s.at[here], pr_send.at[j], pr_recv.at[j], (peer // NH, peer % NH, h)
        )

    for n in range(GROUP):
        prod_s[n] = dot(og_s[n * part:(n + 1) * part], ag_s[h], ((1,), (1,))).astype(BF16)
    for j in range(1, GROUP):
        part_copy(j).start()

    def backward_column(slot):
        factors = [
            jnp.exp2((mb_s[slot, c] - m_s[c]) * EXPO) * rl_s[c] for c in range(SPAN)
        ]
        for t in range(SPAN):
            rows = slice(t * TILE, (t + 1) * TILE)
            lo, hi = span_of(t)
            vals = jnp.concatenate([kv_s[slot, 1, rows], ones_cols], axis=1)
            for c in range(lo, hi):
                n = PAIR_AT[t, c]
                grad = dot(vals, dot_s[c])
                probs = p_s[slot, n].astype(F32) * factors[c]
                ps_s[n] = probs.astype(BF16)
                ds_s[n] = (probs * grad).astype(BF16)
            near = slice(lo * TILE, hi * TILE)
            many_ds = jnp.concatenate([ds_s[PAIR_AT[t, c]] for c in range(lo, hi)], axis=1)
            many_ps = jnp.concatenate([ps_s[PAIR_AT[t, c]] for c in range(lo, hi)], axis=1)
            acc_s[0, rows] = dot(many_ds, q_s[near]) * SCALE
            acc_s[1, rows] = dot(many_ps, do_s[near])
        for c in range(SPAN):
            lo, hi = span_of(c)
            many = jnp.concatenate([ds_s[PAIR_AT[t, c]] for t in range(lo, hi)], axis=0)
            dqt_s[c] += dot(kt_s[slot, :, lo * TILE:hi * TILE], many)

    back = {
        7: (rx_s.at[0], 0, dev_lo, both(inner, has_lo)),
        8: (rx_s.at[1], 1, dev_hi, both(inner, has_hi)),
        5: (rp_s.at[1], 2, dev_partner, has_lo),
        6: (rp_s.at[2], 3, dev_partner, has_hi),
        3: (rz_s.at[0], 4, dev_lo, has_lo),
        4: (rz_s.at[1], 5, dev_hi, has_hi),
        2: (ry_s, 6, dev_cross, inner),
        1: (rp_s.at[0], 7, dev_partner, yes),
    }
    back_arrives = {
        7: both(inner, has_hi), 8: both(inner, has_lo), 5: has_lo, 6: has_hi,
        3: has_hi, 4: has_lo, 2: inner, 1: yes,
    }

    def back_copy(slot):
        target, index, device, _ = back[slot]
        return remote(send_s.at[slot - 1], target, b_send.at[slot - 1], b_recv.at[index], device)

    def add_arrived(slot):
        @pl.when(back_arrives[slot])
        def _():
            back_copy(slot).wait_recv()
            acc_s[...] += back[slot][0][...].astype(F32)

    needs = {7: (), 8: (), 5: (), 6: (), 3: (5,), 4: (6,), 2: (7, 8), 1: ()}

    def backward_step(i, carry):
        slot = chosen(i, BACK_ORDER)

        @pl.when(i == 4)
        def _():
            relay((0,), (3, 4))
            relay((1, 2), (5, 6))

        @pl.when(i == 7)
        def _():
            relay((3, 4), (7, 8))

        @pl.when(exists(slot))
        def _():
            backward_column(slot)

        for n in range(1, SLOTS):
            @pl.when(both(slot == n, back[n][3]))
            def _():
                for source in needs[n]:
                    add_arrived(source)
                send_s[n - 1] = acc_s[...].astype(BF16)
                back_copy(n).start()

        return carry

    lax.fori_loop(0, SLOTS, backward_step, 0)

    for c in range(SPAN):
        rows = slice(c * TILE, (c + 1) * TILE)
        dq_ref[rows] = (dqt_s[c] * SCALE).T.astype(BF16)

    loads_w = w_s[pl.ds(pl.multiple_of(h * share, share), share)]
    wgat_s[h] = loads_w
    for j in range(1, HEADS):
        weight_copy(j).wait_recv()
    relay((5, 6, 7, 8), ())
    weights = jnp.concatenate([wgat_s[n] for n in range(HEADS)], axis=1)
    everyone = jnp.concatenate([ag_s[n] for n in range(HEADS)], axis=0)
    mixed_ref[...] = dot(weights, everyone).astype(BF16).reshape(share, SPAN, TILE)

    red_s[here] = prod_s[here]
    for j in range(1, GROUP):
        part_copy(j).wait_recv()
    total = red_s[0].astype(F32)
    for n in range(1, GROUP):
        total = total + red_s[n].astype(F32)
    wg_ref[...] = total

    for slot in (1, 4, 3, 2):
        add_arrived(slot)
    dk_ref[...] = acc_s[0].astype(BF16)
    dv_ref[...] = acc_s[1].astype(BF16)

    for n in range(len(hops)):
        @pl.when(hops[n][3])
        def _():
            for copy in hop_copies(n):
                copy.wait_send()
    for slot in range(1, SLOTS):
        @pl.when(back[slot][3])
        def _():
            back_copy(slot).wait_send()
    for j in range(1, HEADS):
        weight_copy(j).wait_send()
    for n in range(len(gathers)):
        gather_copy(n).wait_send()
    for j in range(1, GROUP):
        part_copy(j).wait_send()


def hand_over(*refs):
    sources, targets, staged, sem = refs[:5], refs[5:10], refs[10:15], refs[15]
    reads = [pltpu.make_async_copy(sources[i], staged[i], sem.at[i]) for i in range(5)]
    writes = [pltpu.make_async_copy(staged[i], targets[i], sem.at[i + 5]) for i in range(5)]
    for read in reads:
        read.start()
    for read, write in zip(reads, writes):
        read.wait()
        write.start()
    for write in writes:
        write.wait()


def per_device(queries, key_tiles, values, token_valid, out_weight, out_grad):
    any_spec = pl.BlockSpec(memory_space=pl.ANY)
    vmem_spec = pl.BlockSpec(memory_space=pltpu.VMEM)
    vmem = pltpu.VMEM
    dma = pltpu.SemaphoreType.DMA
    token = jax.ShapeDtypeStruct((TOKENS, HD), BF16)
    pair = (2, TOKENS, HD)
    results = pl.pallas_call(
        kernel,
        out_shape=(
            jax.ShapeDtypeStruct((D // HEADS, SPAN, TILE), BF16),
            token, token, token,
            jax.ShapeDtypeStruct((D // GROUP, HD), F32),
        ),
        in_specs=[any_spec, any_spec, any_spec, vmem_spec, any_spec, any_spec],
        out_specs=(vmem_spec,) * 5,
        scratch_shapes=[
            vmem((TOKENS, HD), BF16),
            vmem((SLOTS,) + pair, BF16),
            vmem((SLOTS, HD, TOKENS), BF16),
            vmem((SLOTS, HD, TOKENS), BF16),
            vmem((TOKENS, HD), BF16),
            vmem((D, HD), BF16),
            vmem((D, SPAN, TILE), BF16),
            vmem((D, TOKENS), BF16),
            vmem((SPAN, 2 * HD, TILE), BF16),
            vmem((TOKENS, HD), BF16),
            vmem((SPAN, 2 * HD, TILE), BF16),
            vmem((SLOTS, len(PAIRS), TILE, TILE), BF16),
            vmem((len(PAIRS), TILE, TILE), BF16),
            vmem((len(PAIRS), TILE, TILE), BF16),
            vmem((SPAN, HD + 16, TILE), F32),
            vmem((SPAN, 1, TILE), F32),
            vmem((SLOTS, SPAN, 1, TILE), F32),
            vmem((SPAN, 1, TILE), F32),
            vmem((SPAN, HD, TILE), F32),
            vmem(pair, F32),
            vmem((SLOTS - 1,) + pair, BF16),
            vmem((3,) + pair, BF16),
            vmem((2,) + pair, BF16),
            vmem((2,) + pair, BF16),
            vmem(pair, BF16),
            vmem((HEADS, HD, TOKENS), BF16),
            vmem((HEADS, D // HEADS, HD), BF16),
            vmem((GROUP, D // GROUP, HD), BF16),
            vmem((GROUP, D // GROUP, HD), BF16),
            dma((5,)), dma((8, 2)), dma((SLOTS, 2)), dma((SLOTS - 1,)), dma((SLOTS - 1,)),
            dma((9,)), dma((9,)), dma((HEADS,)), dma((HEADS,)), dma((GROUP,)), dma((GROUP,)),
        ],
        compiler_params=pltpu.CompilerParams(
            collective_id=0, has_side_effects=True, vmem_limit_bytes=60 * 1024 * 1024
        ),
    )(
        queries.reshape(TOKENS, HD),
        key_tiles.reshape(TOKENS, HD),
        values.reshape(TOKENS, HD),
        token_valid,
        out_weight,
        out_grad.reshape(D, SPAN, TILE),
    )
    mixed, dq, dk, dv, wg = pl.pallas_call(
        hand_over,
        out_shape=[jax.ShapeDtypeStruct(r.shape, r.dtype) for r in results],
        in_specs=[any_spec] * 5,
        out_specs=[any_spec] * 5,
        scratch_shapes=[vmem(r.shape, r.dtype) for r in results] + [dma((10,))],
    )(*results)
    tile_shape = (1, 1, 1, SPAN, TILE, HD)
    return (
        mixed.reshape(D // HEADS, 1, 1, SPAN, TILE),
        dq.reshape(tile_shape),
        dk.reshape(tile_shape),
        dv.reshape(tile_shape),
        wg,
    )


def solution(mesh):
    placed = (
        P("head", "tm", "height", None, None, None),
        P("head", "tm", "height", None, None, None),
        P("head", "tm", "height", None, None, None),
        P(),
        P(None, "head"),
        P(None, "tm", "height", None, None),
    )
    return jax.shard_map(
        per_device,
        mesh=mesh,
        in_specs=placed,
        out_specs=(
            P("head", "tm", "height", None, None),
            P("head", "tm", "height", None, None, None),
            P("head", "tm", "height", None, None, None),
            P("head", "tm", "height", None, None, None),
            P(("tm", "height"), "head"),
        ),
        check_vma=False,
    )
```

```python
import functools
import math

import jax
import jax.numpy as jnp
from jax import lax
from jax.experimental import pallas as pl
from jax.experimental.pallas import tpu as pltpu
from jax.sharding import PartitionSpec as P

MESH = pl.DeviceIdType.MESH
F32 = jnp.float32
BF16 = jnp.bfloat16

TILE = 256
SPAN = 4
TOKENS = TILE * SPAN
HD = 128
D = 1536
HEADS = 8
NT = 4
NH = 4
GROUP = NT * NH
SCALE = 1.0 / math.sqrt(HD)
EXPO = SCALE * math.log2(math.e)
LOWEST = -1e30

SLOTS = 9
HALF = TOKENS // 2
BACK_ORDER = (7, 8, 5, 6, 2, 3, 4, 1, 0)

PAIRS = [(k, q) for k in range(SPAN) for q in range(SPAN) if abs(k - q) <= 1]
PAIR_AT = {pair: i for i, pair in enumerate(PAIRS)}


def dot(lhs, rhs, dims=((1,), (0,))):
    return lax.dot_general(lhs, rhs, (dims, ((), ())), preferred_element_type=F32)


def chosen(index, table):
    value = jnp.int32(table[0])
    for at, entry in enumerate(table):
        value = jnp.where(index == at, jnp.int32(entry), value)
    return value


def kernel(
    q_ref, k_ref, v_ref, tv_ref, w_ref, og_ref,
    mixed_ref, dq_ref, dk_ref, dv_ref, wg_ref,
    q_s, kv_s, kt_s, vt_s, mask_s, w_s, raw_s, og_s,
    qt_s, do_s, dot_s, p_s, ps_s, ds_s, att_s, m_s, mb_s, rl_s, dqt_s,
    acc_s, send_s, rp_s, rz_s, rx_s, rd_s, ry_s, ag_s, wgat_s, prod_s, pair_s, sum_s, red_s,
    loc_sem, f_send, f_recv, b_send, b_recv, ag_send, ag_recv, wt_send, wt_recv, pr_send, pr_recv,
):
    a = lax.axis_index("tm")
    b = lax.axis_index("height")
    h = lax.axis_index("head")
    inner = jnp.logical_or(a == 1, a == 2)
    has_lo = b > 0
    has_hi = b < NH - 1
    partner = a + 1 - 2 * (a % 2)
    cross = NT - 1 - a
    here = a * NH + b
    dev_partner = (partner, b, h)
    dev_cross = (cross, b, h)
    dev_lo = (a, b - 1, h)
    dev_hi = (a, b + 1, h)
    both = jnp.logical_and

    loads = [
        pltpu.make_async_copy(src, dst, loc_sem.at[i])
        for i, (src, dst) in enumerate(
            [(q_ref, q_s), (w_ref, w_s), (og_ref, raw_s)]
            + [
                (ref.at[pl.ds(part * HALF, HALF)], kv_s.at[0, part, kind])
                for part in range(2) for kind, ref in enumerate((k_ref, v_ref))
            ]
        )
    ]
    for n in (3, 4, 5, 6, 0, 1, 2):
        loads[n].start()

    barrier = pltpu.get_barrier_semaphore()
    for j in range(1, GROUP):
        peer = (here + j) % GROUP
        pl.semaphore_signal(barrier, inc=1, device_id=(peer // NH, peer % NH, h), device_id_type=MESH)
    for j in range(1, HEADS):
        pl.semaphore_signal(barrier, inc=1, device_id=(a, b, (h + j) % HEADS), device_id_type=MESH)
    pl.semaphore_wait(barrier, GROUP - 1 + HEADS - 1)

    def remote(src, dst, send, recv, device):
        return pltpu.make_async_remote_copy(
            src_ref=src, dst_ref=dst, send_sem=send, recv_sem=recv, device_id=device, device_id_type=MESH
        )

    yes = a >= 0
    hops = [
        (0, 3, dev_hi, has_hi, (0, 1)),
        (0, 4, dev_lo, has_lo, (0, 1)),
        (0, 2, dev_cross, inner, (0, 1)),
        (0, 1, dev_partner, yes, (0, 1)),
        (3, 5, dev_partner, has_lo, (0, 1)),
        (4, 6, dev_partner, has_hi, (0, 1)),
        (2, 7, dev_hi, both(inner, has_hi), (1,)),
        (2, 8, dev_lo, both(inner, has_lo), (1,)),
        (3, 7, dev_cross, both(inner, has_lo), (0,)),
        (4, 8, dev_cross, both(inner, has_hi), (0,)),
    ]
    arrives = [yes, yes, inner, has_lo, has_hi, has_lo, has_hi, both(inner, has_lo), both(inner, has_hi)]

    def hop_copy(n, part):
        source, target, device, _, _ = hops[n]
        return remote(
            kv_s.at[source, part], kv_s.at[target, part], f_send.at[n, part], f_recv.at[target, part], device
        )

    def start_hop(n, part):
        @pl.when(hops[n][3])
        def _():
            hop_copy(n, part).start()

    def wait_unit(slot, part):
        @pl.when(arrives[slot])
        def _():
            remote(
                kv_s.at[slot, part], kv_s.at[slot, part], f_send.at[0, 0], f_recv.at[slot, part], dev_partner
            ).wait_recv()

    for n in range(3, 7):
        loads[n].wait()
    for part in range(2):
        for n in range(4):
            start_hop(n, part)

    share = D // HEADS

    def weight_copy(j):
        peer = (h + j) % HEADS
        return remote(
            w_ref.at[pl.ds(pl.multiple_of(peer * share, share), share)], wgat_s.at[h],
            wt_send.at[j], wt_recv.at[j], (a, b, peer),
        )

    for j in range(1, HEADS):
        weight_copy(j).start()

    loads[0].wait()
    first_row = (lax.broadcasted_iota(jnp.int32, (HD, TILE), 0) == 0).astype(BF16)
    for c in range(SPAN):
        rows = slice(c * TILE, (c + 1) * TILE)
        qt_s[c, :HD] = q_s[rows].T
        qt_s[c, HD:] = first_row
        m_s[c] = jnp.full((1, TILE), LOWEST, F32)
        att_s[c] = jnp.zeros((HD + 16, TILE), F32)
    ones_rows = jnp.ones((16, TOKENS), BF16)
    ones_cols = jnp.ones((TILE, HD), BF16)

    def keys_of(c, tiles):
        near = [t for t in tiles if abs(t - c) <= 1]
        return (near[0], near[-1] + 1) if near else (0, 0)

    def tile_of(ref, slot, kind, t):
        return ref[slot, t // 2, kind, (t % 2) * TILE:(t % 2 + 1) * TILE]

    def queries_of(t):
        return max(0, t - 1), min(SPAN, t + 2)

    def near_queries(tiles):
        return [c for c in range(SPAN) if keys_of(c, tiles)[1]]

    def place(slot):
        frame = chosen(slot, (0, 1, 2, 0, 0, 1, 1, 2, 2))
        frame = jnp.where(frame == 0, a, jnp.where(frame == 1, partner, cross))
        row = b + chosen(slot, (0, 0, 0, -1, 1, -1, 1, -1, 1))
        return frame, row

    def exists(slot):
        far = chosen(slot, (0, 0, 1, 0, 0, 0, 0, 1, 1))
        row = b + chosen(slot, (0, 0, 0, -1, 1, -1, 1, -1, 1))
        near = both(row >= 0, row < NH)
        return both(near, jnp.logical_or(far == 0, inner))

    def forward_unit(slot, tiles):
        frame, row = place(slot)
        for t in tiles:
            rows = slice(t * TILE, (t + 1) * TILE)
            kt_s[slot, :, rows] = tile_of(kv_s, slot, 0, t).T
            vt_s[slot, :, rows] = tile_of(kv_s, slot, 1, t).T
            valid = tv_ref[frame, row, t:t + 1, :]
            bias = jnp.where(valid > 0, 0.0, LOWEST)
            mask_s[rows] = jnp.broadcast_to(bias, (HD, TILE)).T.astype(BF16)
        shrink = {}
        for c in near_queries(tiles):
            lo, hi = keys_of(c, tiles)
            keys = jnp.concatenate([tile_of(kv_s, slot, 0, t) for t in range(lo, hi)], axis=0)
            keys = jnp.concatenate([keys, mask_s[lo * TILE:hi * TILE]], axis=1)
            scores = dot(keys, qt_s[c])
            old = m_s[c]
            new = jnp.maximum(old, jnp.max(scores, axis=0, keepdims=True))
            weights = jnp.exp2((scores - new) * EXPO).astype(BF16)
            for t in range(lo, hi):
                p_s[slot, PAIR_AT[t, c]] = weights[(t - lo) * TILE:(t - lo + 1) * TILE]
            shrink[c] = jnp.exp2((old - new) * EXPO)
            m_s[c] = new
            for part in sorted({t // 2 for t in range(lo, hi)}):
                mb_s[slot, part, c] = new
        for c in near_queries(tiles):
            lo, hi = keys_of(c, tiles)
            rows = slice(lo * TILE, hi * TILE)
            vals = jnp.concatenate([vt_s[slot, :, rows], ones_rows[:, rows]], axis=0)
            weights = jnp.concatenate([p_s[slot, PAIR_AT[t, c]] for t in range(lo, hi)], axis=0)
            att_s[c] = att_s[c] * shrink[c] + dot(vals, weights)

    def grad_attended():
        for load in loads[1:3]:
            load.wait()
        for n in range(0, D, HD):
            og_s[n:n + HD] = raw_s[n:n + HD].reshape(HD, TOKENS)
        for c in range(SPAN):
            rows = slice(c * TILE, (c + 1) * TILE)
            grad = dot(w_s[...], og_s[:, rows], ((0,), (0,))).astype(BF16)
            dot_s[c, :HD] = grad
            do_s[rows] = grad.T

    every = tuple(range(SPAN))

    def forward_pass(first, count, tiles, events):
        def step(i, carry):
            for at, waits in events.items():
                @pl.when(i == at - first)
                def _():
                    if at == 1:
                        grad_attended()
                    for source, part, starts in waits:
                        wait_unit(source, part)
                        for n in starts:
                            start_hop(n, part)

            @pl.when(exists(i + first))
            def _():
                forward_unit(i + first, tiles)

            return carry

        lax.fori_loop(0, count, step, 0)

    forward_pass(0, 3, every, {
        1: [(1, 0, ()), (1, 1, ())],
        2: [(3, 0, (4, 8)), (4, 0, (5, 9)), (2, 0, ()), (2, 1, (6, 7))],
    })
    forward_pass(3, 4, (0, 1), {5: [(5, 0, ())], 6: [(6, 0, ())]})
    forward_pass(3, 4, (2, 3), {3: [(3, 1, (4,)), (4, 1, (5,))], 5: [(5, 1, ())], 6: [(6, 1, ())]})
    forward_pass(7, 2, every, {7: [(7, 0, ()), (7, 1, ())], 8: [(8, 0, ()), (8, 1, ())]})

    for c in range(SPAN):
        rows = slice(c * TILE, (c + 1) * TILE)
        inverse = 1.0 / att_s[c, HD:HD + 1]
        rl_s[c] = inverse
        attended = (att_s[c, :HD] * inverse).astype(BF16)
        ag_s[h, :, rows] = attended
        delta = jnp.sum(dot_s[c, :HD].astype(F32) * attended.astype(F32), axis=0, keepdims=True)
        high = delta.astype(BF16).astype(F32)
        middle = (delta - high).astype(BF16).astype(F32)
        low = delta - high - middle
        index = lax.broadcasted_iota(jnp.int32, (HD, TILE), 0)
        extra = jnp.where(index == 0, -high, jnp.where(index == 1, -middle, jnp.where(index == 2, -low, 0.0)))
        dot_s[c, HD:] = extra.astype(BF16)
        dqt_s[c] = jnp.zeros((HD, TILE), F32)

    side = h + 1 - 2 * (h % 2)
    up, down = (h + 2) % HEADS, (h + HEADS - 2) % HEADS
    side_up, side_down = (side + 2) % HEADS, (side + HEADS - 2) % HEADS
    half = HD // 2
    low_half, high_half = pl.ds(0, half), pl.ds(half, half)
    gathers = [
        (ag_s.at[h], side),
        (ag_s.at[h], up),
        (ag_s.at[h], down),
        (ag_s.at[side], up),
        (ag_s.at[side], down),
        (ag_s.at[down, low_half], up),
        (ag_s.at[up, high_half], down),
        (ag_s.at[side_down, low_half], up),
        (ag_s.at[side_up, high_half], down),
    ]

    def gather_copy(n):
        block, peer = gathers[n]
        return remote(block, block, ag_send.at[n], ag_recv.at[n], (a, b, peer))

    def relay(waits, starts):
        for n in waits:
            gather_copy(n).wait_recv()
        for n in starts:
            gather_copy(n).start()

    relay((), (0, 1, 2))

    piece = D // GROUP
    core = a % 2
    chips = GROUP // 2
    chip = (a // 2) * NH + b

    def pair_copy():
        return remote(prod_s.at[1 - core], pair_s, pr_send.at[0], pr_recv.at[0], dev_partner)

    def part_copy(j):
        peer = (chip + j) % chips
        return remote(
            sum_s.at[peer], red_s.at[chip], pr_send.at[j], pr_recv.at[j], ((peer // NH) * 2 + core, peer % NH, h)
        )

    def weight_product():
        for n in range(GROUP):
            frame, row = n // NH, n % NH
            value = dot(og_s[n * piece:(n + 1) * piece], ag_s[h], ((1,), (1,)))
            prod_s[frame % 2, (frame // 2) * NH + row] = value.astype(BF16)
        pair_copy().start()

    def weight_parts():
        pair_copy().wait_recv()
        sum_s[...] = (prod_s[core].astype(F32) + pair_s[...].astype(F32)).astype(BF16)
        for j in range(1, chips):
            part_copy(j).start()

    def backward_unit(slot):
        factors = {
            (part, c): jnp.exp2((mb_s[slot, part, c] - m_s[c]) * EXPO) * rl_s[c]
            for part in range(2) for c in near_queries((2 * part, 2 * part + 1))
        }
        for t in every:
            vals = jnp.concatenate([tile_of(kv_s, slot, 1, t), ones_cols], axis=1)
            for c in range(*queries_of(t)):
                n = PAIR_AT[t, c]
                grad = dot(vals, dot_s[c])
                probs = p_s[slot, n].astype(F32) * factors[t // 2, c]
                ps_s[n] = probs.astype(BF16)
                ds_s[n] = (probs * grad).astype(BF16)
        for t in every:
            rows = slice((t % 2) * TILE, (t % 2 + 1) * TILE)
            lo, hi = queries_of(t)
            near = slice(lo * TILE, hi * TILE)
            many_ds = jnp.concatenate([ds_s[PAIR_AT[t, c]] for c in range(lo, hi)], axis=1)
            many_ps = jnp.concatenate([ps_s[PAIR_AT[t, c]] for c in range(lo, hi)], axis=1)
            send_s[slot, t // 2, 0, rows] = (dot(many_ds, q_s[near]) * SCALE).astype(BF16)
            send_s[slot, t // 2, 1, rows] = dot(many_ps, do_s[near]).astype(BF16)
        for c in range(SPAN):
            lo, hi = keys_of(c, every)
            many = jnp.concatenate([ds_s[PAIR_AT[t, c]] for t in range(lo, hi)], axis=0)
            dqt_s[c] += dot(kt_s[slot, :, lo * TILE:hi * TILE], many)

    back = {
        (7, 0): (rd_s.at[0], 0, dev_cross, both(inner, has_lo), both(inner, has_lo)),
        (8, 0): (rd_s.at[1], 1, dev_cross, both(inner, has_hi), both(inner, has_hi)),
        (7, 1): (rx_s.at[0], 2, dev_lo, both(inner, has_lo), both(inner, has_hi)),
        (8, 1): (rx_s.at[1], 3, dev_hi, both(inner, has_hi), both(inner, has_lo)),
    }
    for part in range(2):
        at = 4 + 6 * part
        back[5, part] = (rp_s.at[1, part], at, dev_partner, has_lo, has_lo)
        back[6, part] = (rp_s.at[2, part], at + 1, dev_partner, has_hi, has_hi)
        back[3, part] = (rz_s.at[0, part], at + 2, dev_lo, has_lo, has_hi)
        back[4, part] = (rz_s.at[1, part], at + 3, dev_hi, has_hi, has_lo)
        back[2, part] = (ry_s.at[part], at + 4, dev_cross, inner, inner)
        back[1, part] = (rp_s.at[0, part], at + 5, dev_partner, yes, yes)
    needs = {key: () for key in back}
    needs[3, 0], needs[4, 0] = ((5, 0), (7, 0)), ((6, 0), (8, 0))
    needs[3, 1], needs[4, 1] = ((5, 1),), ((6, 1),)
    needs[2, 1] = ((7, 1), (8, 1))

    def back_copy(key):
        slot, part = key
        target, index, device, _, _ = back[key]
        return remote(send_s.at[slot, part], target, b_send.at[index], b_recv.at[index], device)

    def merge(key, source):
        @pl.when(back[source][4])
        def _():
            back_copy(source).wait_recv()
            slot, part = key
            arrived = back[source][0][...].astype(F32)
            send_s[slot, part] = (send_s[slot, part].astype(F32) + arrived).astype(BF16)

    def backward_step(i, carry):
        slot = chosen(i, BACK_ORDER)

        @pl.when(i == 4)
        def _():
            relay((0,), (3, 4))
            relay((1, 2), (5, 6))
            weight_product()

        @pl.when(i == 6)
        def _():
            weight_parts()

        @pl.when(i == 7)
        def _():
            relay((3, 4), (7, 8))

        @pl.when(exists(slot))
        def _():
            backward_unit(slot)

        for n in range(1, SLOTS):
            @pl.when(slot == n)
            def _():
                for part in range(2):
                    @pl.when(back[n, part][3])
                    def _():
                        for source in needs[n, part]:
                            merge((n, part), source)
                        back_copy((n, part)).start()

        return carry

    lax.fori_loop(0, SLOTS, backward_step, 0)

    for c in range(SPAN):
        rows = slice(c * TILE, (c + 1) * TILE)
        dq_ref[rows] = (dqt_s[c] * SCALE).T.astype(BF16)

    loads_w = w_s[pl.ds(pl.multiple_of(h * share, share), share)]
    wgat_s[h] = loads_w
    for j in range(1, HEADS):
        weight_copy(j).wait_recv()
    relay((5, 6, 7, 8), ())
    weights = jnp.concatenate([wgat_s[n] for n in range(HEADS)], axis=1)
    everyone = jnp.concatenate([ag_s[n] for n in range(HEADS)], axis=0)
    mixed_ref[...] = dot(weights, everyone).astype(BF16).reshape(share, SPAN, TILE)

    red_s[chip] = sum_s[chip]
    for j in range(1, chips):
        part_copy(j).wait_recv()
    total = red_s[0].astype(F32)
    for n in range(1, chips):
        total = total + red_s[n].astype(F32)
    wg_ref[...] = total

    for part in range(2):
        back_copy((1, part)).wait_recv()
        acc_s[part] = send_s[0, part].astype(F32) + rp_s[0, part].astype(F32)
    for part in range(2):
        for source in (4, 3, 2):
            @pl.when(back[source, part][4])
            def _():
                back_copy((source, part)).wait_recv()
                acc_s[part] += back[source, part][0][...].astype(F32)
        rows = slice(part * HALF, (part + 1) * HALF)
        dk_ref[rows] = acc_s[part, 0].astype(BF16)
        dv_ref[rows] = acc_s[part, 1].astype(BF16)

    for n in range(len(hops)):
        @pl.when(hops[n][3])
        def _():
            for part in hops[n][4]:
                hop_copy(n, part).wait_send()
    for key, (_, _, _, sends, _) in back.items():
        @pl.when(sends)
        def _():
            back_copy(key).wait_send()
    for j in range(1, HEADS):
        weight_copy(j).wait_send()
    for n in range(len(gathers)):
        gather_copy(n).wait_send()
    pair_copy().wait_send()
    for j in range(1, chips):
        part_copy(j).wait_send()


def hand_over(*refs):
    sources, targets, staged, sem = refs[:5], refs[5:10], refs[10:15], refs[15]
    reads = [pltpu.make_async_copy(sources[i], staged[i], sem.at[i]) for i in range(5)]
    writes = [pltpu.make_async_copy(staged[i], targets[i], sem.at[i + 5]) for i in range(5)]
    for read in reads:
        read.start()
    for read, write in zip(reads, writes):
        read.wait()
        write.start()
    for write in writes:
        write.wait()


def per_device(queries, key_tiles, values, token_valid, out_weight, out_grad):
    any_spec = pl.BlockSpec(memory_space=pl.ANY)
    vmem_spec = pl.BlockSpec(memory_space=pltpu.VMEM)
    vmem = pltpu.VMEM
    dma = pltpu.SemaphoreType.DMA
    token = jax.ShapeDtypeStruct((TOKENS, HD), BF16)
    unit = (2, HALF, HD)
    pieces = (GROUP // 2, D // GROUP, HD)
    results = pl.pallas_call(
        kernel,
        out_shape=(
            jax.ShapeDtypeStruct((D // HEADS, SPAN, TILE), BF16),
            token, token, token,
            jax.ShapeDtypeStruct((D // GROUP, HD), F32),
        ),
        in_specs=[any_spec, any_spec, any_spec, vmem_spec, any_spec, any_spec],
        out_specs=(vmem_spec,) * 5,
        scratch_shapes=[
            vmem((TOKENS, HD), BF16),
            vmem((SLOTS, 2) + unit, BF16),
            vmem((SLOTS, HD, TOKENS), BF16),
            vmem((SLOTS, HD, TOKENS), BF16),
            vmem((TOKENS, HD), BF16),
            vmem((D, HD), BF16),
            vmem((D, SPAN, TILE), BF16),
            vmem((D, TOKENS), BF16),
            vmem((SPAN, 2 * HD, TILE), BF16),
            vmem((TOKENS, HD), BF16),
            vmem((SPAN, 2 * HD, TILE), BF16),
            vmem((SLOTS, len(PAIRS), TILE, TILE), BF16),
            vmem((len(PAIRS), TILE, TILE), BF16),
            vmem((len(PAIRS), TILE, TILE), BF16),
            vmem((SPAN, HD + 16, TILE), F32),
            vmem((SPAN, 1, TILE), F32),
            vmem((SLOTS, 2, SPAN, 1, TILE), F32),
            vmem((SPAN, 1, TILE), F32),
            vmem((SPAN, HD, TILE), F32),
            vmem((2,) + unit, F32),
            vmem((SLOTS, 2) + unit, BF16),
            vmem((3, 2) + unit, BF16),
            vmem((2, 2) + unit, BF16),
            vmem((2,) + unit, BF16),
            vmem((2,) + unit, BF16),
            vmem((2,) + unit, BF16),
            vmem((HEADS, HD, TOKENS), BF16),
            vmem((HEADS, D // HEADS, HD), BF16),
            vmem((2,) + pieces, BF16),
            vmem(pieces, BF16),
            vmem(pieces, BF16),
            vmem(pieces, BF16),
            dma((7,)), dma((10, 2)), dma((SLOTS, 2)), dma((16,)), dma((16,)),
            dma((9,)), dma((9,)), dma((HEADS,)), dma((HEADS,)), dma((GROUP // 2,)), dma((GROUP // 2,)),
        ],
        compiler_params=pltpu.CompilerParams(
            collective_id=0, has_side_effects=True, vmem_limit_bytes=60 * 1024 * 1024
        ),
    )(
        queries.reshape(TOKENS, HD),
        key_tiles.reshape(TOKENS, HD),
        values.reshape(TOKENS, HD),
        token_valid,
        out_weight,
        out_grad.reshape(D, SPAN, TILE),
    )
    mixed, dq, dk, dv, wg = pl.pallas_call(
        hand_over,
        out_shape=[jax.ShapeDtypeStruct(r.shape, r.dtype) for r in results],
        in_specs=[any_spec] * 5,
        out_specs=[any_spec] * 5,
        scratch_shapes=[vmem(r.shape, r.dtype) for r in results] + [dma((10,))],
    )(*results)
    tile_shape = (1, 1, 1, SPAN, TILE, HD)
    return (
        mixed.reshape(D // HEADS, 1, 1, SPAN, TILE),
        dq.reshape(tile_shape),
        dk.reshape(tile_shape),
        dv.reshape(tile_shape),
        wg,
    )


def solution(mesh):
    placed = (
        P("head", "tm", "height", None, None, None),
        P("head", "tm", "height", None, None, None),
        P("head", "tm", "height", None, None, None),
        P(),
        P(None, "head"),
        P(None, "tm", "height", None, None),
    )
    return jax.shard_map(
        per_device,
        mesh=mesh,
        in_specs=placed,
        out_specs=(
            P("head", "tm", "height", None, None),
            P("head", "tm", "height", None, None, None),
            P("head", "tm", "height", None, None, None),
            P("head", "tm", "height", None, None, None),
            P(("tm", "height"), "head"),
        ),
        check_vma=False,
    )
```

```python
import functools
import math

import jax
import jax.numpy as jnp
from jax import lax
from jax.experimental import pallas as pl
from jax.experimental.pallas import tpu as pltpu
from jax.sharding import PartitionSpec as P

MESH = pl.DeviceIdType.MESH
F32 = jnp.float32
BF16 = jnp.bfloat16

TILE = 256
SPAN = 4
TOKENS = TILE * SPAN
HD = 128
D = 1536
HEADS = 8
NT = 4
NH = 4
GROUP = NT * NH
SCALE = 1.0 / math.sqrt(HD)
EXPO = SCALE * math.log2(math.e)
LOWEST = -1e30

SLOTS = 9
HALF = TOKENS // 2
LAST_ORDER = (2, 3, 4, 1, 0)

PAIRS = [(k, q) for k in range(SPAN) for q in range(SPAN) if abs(k - q) <= 1]
PAIR_AT = {pair: i for i, pair in enumerate(PAIRS)}


def dot(lhs, rhs, dims=((1,), (0,))):
    return lax.dot_general(lhs, rhs, (dims, ((), ())), preferred_element_type=F32)


def chosen(index, table):
    value = jnp.int32(table[0])
    for at, entry in enumerate(table):
        value = jnp.where(index == at, jnp.int32(entry), value)
    return value


def kernel(
    q_ref, k_ref, v_ref, tv_ref, w_ref, og_ref,
    mixed_ref, dq_ref, dk_ref, dv_ref, wg_ref,
    mixed_s, most_s, dq_s, dk_s, dv_s, wg_s, tv_s,
    q_s, kv_s, kt_s, vt_s, mask_s, w_s, raw_s, og_s,
    qt_s, do_s, dot_s, p_s, ps_s, ds_s, att_s, m_s, mb_s, rl_s, dqt_s,
    acc_s, send_s, rp_s, rz_s, rx_s, rd_s, rw_s, ry_s, ag_s, wgat_s, prod_s, pair_s, sum_s, red_s,
    loc_sem, out_sem, f_send, f_recv, b_send, b_recv, ag_send, ag_recv, wt_send, wt_recv, pr_send, pr_recv,
):
    a = lax.axis_index("tm")
    b = lax.axis_index("height")
    h = lax.axis_index("head")
    inner = jnp.logical_or(a == 1, a == 2)
    has_lo = b > 0
    has_hi = b < NH - 1
    partner = a + 1 - 2 * (a % 2)
    cross = NT - 1 - a
    here = a * NH + b
    dev_partner = (partner, b, h)
    dev_cross = (cross, b, h)
    dev_lo = (a, b - 1, h)
    dev_hi = (a, b + 1, h)
    both = jnp.logical_and

    loads = [
        pltpu.make_async_copy(src, dst, loc_sem.at[i])
        for i, (src, dst) in enumerate(
            [(q_ref, q_s), (w_ref, w_s), (og_ref, raw_s)]
            + [
                (ref.at[pl.ds(part * HALF, HALF)], kv_s.at[0, part, kind])
                for part in range(2) for kind, ref in enumerate((k_ref, v_ref))
            ]
            + [(tv_ref, tv_s)]
        )
    ]
    for n in (3, 4, 5, 6, 0, 7, 1, 2):
        loads[n].start()

    barrier = pltpu.get_barrier_semaphore()
    for j in range(1, GROUP):
        peer = (here + j) % GROUP
        pl.semaphore_signal(barrier, inc=1, device_id=(peer // NH, peer % NH, h), device_id_type=MESH)
    for j in range(1, HEADS):
        pl.semaphore_signal(barrier, inc=1, device_id=(a, b, (h + j) % HEADS), device_id_type=MESH)
    pl.semaphore_wait(barrier, GROUP - 1 + HEADS - 1)

    def remote(src, dst, send, recv, device):
        return pltpu.make_async_remote_copy(
            src_ref=src, dst_ref=dst, send_sem=send, recv_sem=recv, device_id=device, device_id_type=MESH
        )

    yes = a >= 0
    hops = [
        (0, 3, dev_hi, has_hi, (0, 1)),
        (0, 4, dev_lo, has_lo, (0, 1)),
        (0, 2, dev_cross, inner, (0, 1)),
        (0, 1, dev_partner, yes, (0, 1)),
        (3, 5, dev_partner, has_lo, (0, 1)),
        (4, 6, dev_partner, has_hi, (0, 1)),
        (2, 7, dev_hi, both(inner, has_hi), (1,)),
        (2, 8, dev_lo, both(inner, has_lo), (1,)),
        (3, 7, dev_cross, both(inner, has_lo), (0,)),
        (4, 8, dev_cross, both(inner, has_hi), (0,)),
    ]
    arrives = [yes, yes, inner, has_lo, has_hi, has_lo, has_hi, both(inner, has_lo), both(inner, has_hi)]

    def hop_copy(n, part):
        source, target, device, _, _ = hops[n]
        return remote(
            kv_s.at[source, part], kv_s.at[target, part], f_send.at[n, part], f_recv.at[target, part], device
        )

    def start_hop(n, part):
        @pl.when(hops[n][3])
        def _():
            hop_copy(n, part).start()

    def wait_unit(slot, part):
        @pl.when(arrives[slot])
        def _():
            remote(
                kv_s.at[slot, part], kv_s.at[slot, part], f_send.at[0, 0], f_recv.at[slot, part], dev_partner
            ).wait_recv()

    for n in range(3, 7):
        loads[n].wait()
    for part in range(2):
        for n in range(4):
            start_hop(n, part)

    share = D // HEADS

    part_share = share // 2
    core = a % 2

    def weight_rows(peer):
        return pl.ds(pl.multiple_of(peer * share + core * part_share, part_share), part_share)

    def weight_copy(j):
        peer = (h + j) % HEADS
        return remote(
            w_ref.at[weight_rows(peer)], wgat_s.at[core, h], wt_send.at[j], wt_recv.at[j], (a, b, peer)
        )

    def weight_exchange():
        return remote(wgat_s.at[core], wgat_s.at[core], wt_send.at[0], wt_recv.at[0], dev_partner)

    for j in range(1, HEADS):
        weight_copy(j).start()

    loads[0].wait()
    loads[7].wait()
    first_row = (lax.broadcasted_iota(jnp.int32, (HD, TILE), 0) == 0).astype(BF16)
    for c in range(SPAN):
        rows = slice(c * TILE, (c + 1) * TILE)
        qt_s[c, :HD] = q_s[rows].T
        qt_s[c, HD:] = first_row
        m_s[c] = jnp.full((1, TILE), LOWEST, F32)
        att_s[c] = jnp.zeros((HD + 16, TILE), F32)
    ones_rows = jnp.ones((16, TOKENS), BF16)
    ones_cols = jnp.ones((TILE, HD), BF16)

    def keys_of(c, tiles):
        near = [t for t in tiles if abs(t - c) <= 1]
        return (near[0], near[-1] + 1) if near else (0, 0)

    def tile_of(ref, slot, kind, t):
        return ref[slot, t // 2, kind, (t % 2) * TILE:(t % 2 + 1) * TILE]

    def queries_of(t):
        return max(0, t - 1), min(SPAN, t + 2)

    def near_queries(tiles):
        return [c for c in range(SPAN) if keys_of(c, tiles)[1]]

    def place(slot):
        frame = chosen(slot, (0, 1, 2, 0, 0, 1, 1, 2, 2))
        frame = jnp.where(frame == 0, a, jnp.where(frame == 1, partner, cross))
        row = b + chosen(slot, (0, 0, 0, -1, 1, -1, 1, -1, 1))
        return frame, row

    def exists(slot):
        far = chosen(slot, (0, 0, 1, 0, 0, 0, 0, 1, 1))
        row = b + chosen(slot, (0, 0, 0, -1, 1, -1, 1, -1, 1))
        near = both(row >= 0, row < NH)
        return both(near, jnp.logical_or(far == 0, inner))

    def forward_unit(slot, tiles):
        frame, row = place(slot)
        for t in tiles:
            rows = slice(t * TILE, (t + 1) * TILE)
            kt_s[slot, :, rows] = tile_of(kv_s, slot, 0, t).T
            vt_s[slot, :, rows] = tile_of(kv_s, slot, 1, t).T
            valid = tv_s[frame, row, t:t + 1, :]
            bias = jnp.where(valid > 0, 0.0, LOWEST)
            mask_s[rows] = jnp.broadcast_to(bias, (HD, TILE)).T.astype(BF16)
        shrink = {}
        for c in near_queries(tiles):
            lo, hi = keys_of(c, tiles)
            keys = jnp.concatenate([tile_of(kv_s, slot, 0, t) for t in range(lo, hi)], axis=0)
            keys = jnp.concatenate([keys, mask_s[lo * TILE:hi * TILE]], axis=1)
            scores = dot(keys, qt_s[c])
            old = m_s[c]
            new = jnp.maximum(old, jnp.max(scores, axis=0, keepdims=True))
            weights = jnp.exp2((scores - new) * EXPO).astype(BF16)
            for t in range(lo, hi):
                p_s[slot, PAIR_AT[t, c]] = weights[(t - lo) * TILE:(t - lo + 1) * TILE]
            shrink[c] = jnp.exp2((old - new) * EXPO)
            m_s[c] = new
            for part in sorted({t // 2 for t in range(lo, hi)}):
                mb_s[slot, part, c] = new
        for c in near_queries(tiles):
            lo, hi = keys_of(c, tiles)
            rows = slice(lo * TILE, hi * TILE)
            vals = jnp.concatenate([vt_s[slot, :, rows], ones_rows[:, rows]], axis=0)
            weights = jnp.concatenate([p_s[slot, PAIR_AT[t, c]] for t in range(lo, hi)], axis=0)
            att_s[c] = att_s[c] * shrink[c] + dot(vals, weights)

    def grad_attended():
        for load in loads[1:3]:
            load.wait()
        for n in range(0, D, HD):
            og_s[n:n + HD] = raw_s[n:n + HD].reshape(HD, TOKENS)
        for c in range(SPAN):
            rows = slice(c * TILE, (c + 1) * TILE)
            grad = dot(w_s[...], og_s[:, rows], ((0,), (0,))).astype(BF16)
            dot_s[c, :HD] = grad
            do_s[rows] = grad.T

    every = tuple(range(SPAN))

    def forward_pass(first, count, tiles, events):
        def step(i, carry):
            for at, waits in events.items():
                @pl.when(i == at - first)
                def _():
                    if at == 1:
                        grad_attended()
                    for source, part, starts in waits:
                        wait_unit(source, part)
                        for n in starts:
                            start_hop(n, part)

            @pl.when(exists(i + first))
            def _():
                forward_unit(i + first, tiles)

            return carry

        lax.fori_loop(0, count, step, 0)

    forward_pass(0, 2, every, {1: [(1, 0, ()), (1, 1, ())]})
    forward_pass(2, 5, (0, 1), {
        2: [(2, 0, ())],
        3: [(3, 0, (4, 8)), (4, 0, (5, 9))],
        5: [(2, 1, (6, 7)), (5, 0, ())],
        6: [(6, 0, ())],
    })
    forward_pass(2, 5, (2, 3), {3: [(3, 1, (4,)), (4, 1, (5,))], 5: [(5, 1, ())], 6: [(6, 1, ())]})
    forward_pass(7, 2, every, {7: [(7, 0, ()), (7, 1, ())], 8: [(8, 0, ()), (8, 1, ())]})

    for c in range(SPAN):
        rows = slice(c * TILE, (c + 1) * TILE)
        inverse = 1.0 / att_s[c, HD:HD + 1]
        rl_s[c] = inverse
        attended = (att_s[c, :HD] * inverse).astype(BF16)
        ag_s[h, :, rows] = attended
        delta = jnp.sum(dot_s[c, :HD].astype(F32) * attended.astype(F32), axis=0, keepdims=True)
        high = delta.astype(BF16).astype(F32)
        middle = (delta - high).astype(BF16).astype(F32)
        low = delta - high - middle
        index = lax.broadcasted_iota(jnp.int32, (HD, TILE), 0)
        extra = jnp.where(index == 0, -high, jnp.where(index == 1, -middle, jnp.where(index == 2, -low, 0.0)))
        dot_s[c, HD:] = extra.astype(BF16)
        dqt_s[c] = jnp.zeros((HD, TILE), F32)

    side = h + 1 - 2 * (h % 2)
    up, down = (h + 2) % HEADS, (h + HEADS - 2) % HEADS
    side_up, side_down = (side + 2) % HEADS, (side + HEADS - 2) % HEADS
    half = HD // 2
    low_half, high_half = pl.ds(0, half), pl.ds(half, half)
    gathers = [
        (ag_s.at[h], side),
        (ag_s.at[h], up),
        (ag_s.at[h], down),
        (ag_s.at[side], up),
        (ag_s.at[side], down),
        (ag_s.at[down, low_half], up),
        (ag_s.at[up, high_half], down),
        (ag_s.at[side_down, low_half], up),
        (ag_s.at[side_up, high_half], down),
    ]

    def gather_copy(n):
        block, peer = gathers[n]
        return remote(block, block, ag_send.at[n], ag_recv.at[n], (a, b, peer))

    def relay(waits, starts):
        for n in waits:
            gather_copy(n).wait_recv()
        for n in starts:
            gather_copy(n).start()

    relay((), (0, 1, 2))

    piece = D // GROUP
    chips = GROUP // 2
    chip = (a // 2) * NH + b

    def pair_copy():
        return remote(prod_s.at[1 - core], pair_s, pr_send.at[0], pr_recv.at[0], dev_partner)

    def part_copy(j):
        peer = (chip + j) % chips
        return remote(
            sum_s.at[peer], red_s.at[chip], pr_send.at[j], pr_recv.at[j], ((peer // NH) * 2 + core, peer % NH, h)
        )

    def weight_product():
        for n in range(GROUP):
            frame, row = n // NH, n % NH
            value = dot(og_s[n * piece:(n + 1) * piece], ag_s[h], ((1,), (1,)))
            prod_s[frame % 2, (frame // 2) * NH + row] = value.astype(BF16)
        pair_copy().start()

    def weight_parts():
        pair_copy().wait_recv()
        sum_s[...] = (prod_s[core].astype(F32) + pair_s[...].astype(F32)).astype(BF16)
        for j in range(1, chips):
            part_copy(j).start()

    def backward_unit(slot, tiles):
        factors = {
            (part, c): jnp.exp2((mb_s[slot, part, c] - m_s[c]) * EXPO) * rl_s[c]
            for part in sorted({t // 2 for t in tiles}) for c in near_queries((2 * part, 2 * part + 1))
        }
        for t in tiles:
            vals = jnp.concatenate([tile_of(kv_s, slot, 1, t), ones_cols], axis=1)
            for c in range(*queries_of(t)):
                n = PAIR_AT[t, c]
                grad = dot(vals, dot_s[c])
                probs = p_s[slot, n].astype(F32) * factors[t // 2, c]
                ps_s[n] = probs.astype(BF16)
                ds_s[n] = (probs * grad).astype(BF16)
        for t in tiles:
            rows = slice((t % 2) * TILE, (t % 2 + 1) * TILE)
            lo, hi = queries_of(t)
            near = slice(lo * TILE, hi * TILE)
            many_ds = jnp.concatenate([ds_s[PAIR_AT[t, c]] for c in range(lo, hi)], axis=1)
            many_ps = jnp.concatenate([ps_s[PAIR_AT[t, c]] for c in range(lo, hi)], axis=1)
            send_s[slot, t // 2, 0, rows] = (dot(many_ds, q_s[near]) * SCALE).astype(BF16)
            send_s[slot, t // 2, 1, rows] = dot(many_ps, do_s[near]).astype(BF16)
        for c in near_queries(tiles):
            lo, hi = keys_of(c, tiles)
            many = jnp.concatenate([ds_s[PAIR_AT[t, c]] for t in range(lo, hi)], axis=0)
            dqt_s[c] += dot(kt_s[slot, :, lo * TILE:hi * TILE], many)

    back = {
        (7, 0): (rd_s.at[0], 0, dev_cross, both(inner, has_lo), both(inner, has_lo)),
        (8, 0): (rd_s.at[1], 1, dev_cross, both(inner, has_hi), both(inner, has_hi)),
        (7, 1): (rx_s.at[0], 2, dev_lo, both(inner, has_lo), both(inner, has_hi)),
        (8, 1): (rx_s.at[1], 3, dev_hi, both(inner, has_hi), both(inner, has_lo)),
        (7, 2): (rw_s.at[0], 16, dev_lo, both(inner, has_lo), both(inner, has_hi)),
        (8, 2): (rw_s.at[1], 17, dev_hi, both(inner, has_hi), both(inner, has_lo)),
    }
    inside = {0: (0, 0), 2: (0, 1)}

    for part in range(2):
        at = 4 + 6 * part
        back[5, part] = (rp_s.at[1, part], at, dev_partner, has_lo, has_lo)
        back[6, part] = (rp_s.at[2, part], at + 1, dev_partner, has_hi, has_hi)
        back[3, part] = (rz_s.at[0, part], at + 2, dev_lo, has_lo, has_hi)
        back[4, part] = (rz_s.at[1, part], at + 3, dev_hi, has_hi, has_lo)
        back[2, part] = (ry_s.at[part], at + 4, dev_cross, inner, inner)
        back[1, part] = (rp_s.at[0, part], at + 5, dev_partner, yes, yes)
    needs = {key: () for key in back}
    needs[3, 0], needs[4, 0] = ((5, 0), (7, 0)), ((6, 0), (8, 0))
    needs[3, 1], needs[4, 1] = ((5, 1),), ((6, 1),)
    needs[2, 0] = ((7, 2), (8, 2))
    needs[2, 1] = ((7, 1), (8, 1))

    def back_copy(key):
        slot, part = key
        target, index, device, _, _ = back[key]
        source = send_s.at[(slot,) + inside[part]] if slot > 6 and part in inside else send_s.at[slot, part]
        return remote(source, target, b_send.at[index], b_recv.at[index], device)

    def merge(key, source):
        @pl.when(back[source][4])
        def _():
            back_copy(source).wait_recv()
            at = (key[0],) + inside[source[1]] if source[0] > 6 and source[1] in inside else key
            arrived = back[source][0][...].astype(F32)
            send_s[at] = (send_s[at].astype(F32) + arrived).astype(BF16)

    def give_back(key, who):
        @pl.when(both(who, back[key][3]))
        def _():
            for source in needs[key]:
                merge(key, source)
            back_copy(key).start()

    outer = jnp.logical_not(inner)

    def first_step(i, carry):
        slot = jnp.where(inner, 7 + i, 3 + i)

        @pl.when(exists(slot))
        def _():
            backward_unit(slot, every)

        for n in (7, 8):
            @pl.when(i == n - 7)
            def _():
                for part in range(3):
                    give_back((n, part), inner)

        return carry

    lax.fori_loop(0, 2, first_step, 0)

    for part in range(2):
        def partner_step(i, carry):
            if part == 1:
                @pl.when(i == 1)
                def _():
                    relay((0,), (3, 4))

            @pl.when(exists(i + 5))
            def _():
                backward_unit(i + 5, (2 * part, 2 * part + 1))

            for n in (5, 6):
                @pl.when(i == n - 5)
                def _():
                    give_back((n, part), yes)

            return carry

        lax.fori_loop(0, 2, partner_step, 0)
        for n in (3, 4):
            give_back((n, part), outer)

    def last_step(i, carry):
        slot = chosen(i, LAST_ORDER)
        own_side = both(slot >= 3, outer)

        @pl.when(i == 0)
        def _():
            relay((1, 2), (5, 6))

        @pl.when(i == 3)
        def _():
            weight_product()
            wgat_s[core, h] = w_s[weight_rows(h)]
            for j in range(1, HEADS):
                weight_copy(j).wait_recv()
            weight_exchange().start()

        @pl.when(i == 4)
        def _():
            weight_parts()
            relay((3, 4), (7, 8))

        @pl.when(both(exists(slot), jnp.logical_not(own_side)))
        def _():
            backward_unit(slot, every)

        for n in range(1, 5):
            @pl.when(slot == n)
            def _():
                for part in range(2):
                    give_back((n, part), inner if n in (3, 4) else yes)

        return carry

    lax.fori_loop(0, len(LAST_ORDER), last_step, 0)

    for c in range(SPAN):
        rows = slice(c * TILE, (c + 1) * TILE)
        dq_s[rows] = (dqt_s[c] * SCALE).T.astype(BF16)

    stores = [
        pltpu.make_async_copy(src, dst, out_sem.at[i])
        for i, (src, dst) in enumerate(
            [(mixed_s, mixed_ref), (dq_s, dq_ref), (dk_s, dk_ref), (dv_s, dv_ref), (wg_s, wg_ref)]
        )
    ]
    stores[1].start()

    def projected(heads):
        rows = [jnp.concatenate([wgat_s[i, n] for n in heads], axis=1) for i in range(2)]
        return dot(jnp.concatenate(rows, axis=0), jnp.concatenate([ag_s[n] for n in heads], axis=0))

    weight_exchange().wait_recv()
    most_s[...] = projected((h, side, up, down, side_up, side_down))
    for part in range(2):
        back_copy((1, part)).wait_recv()
        acc_s[part] = send_s[0, part].astype(F32) + rp_s[0, part].astype(F32)
    for part in range(2):
        for source in (4, 3, 2):
            @pl.when(back[source, part][4])
            def _():
                back_copy((source, part)).wait_recv()
                acc_s[part] += back[source, part][0][...].astype(F32)
        rows = slice(part * HALF, (part + 1) * HALF)
        dk_s[rows] = acc_s[part, 0].astype(BF16)
        dv_s[rows] = acc_s[part, 1].astype(BF16)

    stores[2].start()
    stores[3].start()

    relay((5, 6, 7, 8), ())
    far = (h + HEADS // 2) % HEADS
    mixed = most_s[...] + projected((far, (side + HEADS // 2) % HEADS))
    mixed_s[...] = mixed.astype(BF16).reshape(share, SPAN, TILE)
    stores[0].start()

    red_s[chip] = sum_s[chip]
    for j in range(1, chips):
        part_copy(j).wait_recv()
    total = red_s[0].astype(F32)
    for n in range(1, chips):
        total = total + red_s[n].astype(F32)
    wg_s[...] = total
    stores[4].start()

    for n in range(len(hops)):
        @pl.when(hops[n][3])
        def _():
            for part in hops[n][4]:
                hop_copy(n, part).wait_send()
    for key, (_, _, _, sends, _) in back.items():
        @pl.when(sends)
        def _():
            back_copy(key).wait_send()
    weight_exchange().wait_send()
    for j in range(1, HEADS):
        weight_copy(j).wait_send()
    for n in range(len(gathers)):
        gather_copy(n).wait_send()
    pair_copy().wait_send()
    for j in range(1, chips):
        part_copy(j).wait_send()
    for store in stores:
        store.wait()


def hand_over(*refs):
    sources, targets, staged, sem = refs[:5], refs[5:10], refs[10:15], refs[15]
    reads = [pltpu.make_async_copy(sources[i], staged[i], sem.at[i]) for i in range(5)]
    writes = [pltpu.make_async_copy(staged[i], targets[i], sem.at[i + 5]) for i in range(5)]
    for read in reads:
        read.start()
    for read, write in zip(reads, writes):
        read.wait()
        write.start()
    for write in writes:
        write.wait()


def per_device(queries, key_tiles, values, token_valid, out_weight, out_grad):
    any_spec = pl.BlockSpec(memory_space=pl.ANY)
    vmem = pltpu.VMEM
    dma = pltpu.SemaphoreType.DMA
    token = jax.ShapeDtypeStruct((TOKENS, HD), BF16)
    unit = (2, HALF, HD)
    pieces = (GROUP // 2, D // GROUP, HD)
    results = pl.pallas_call(
        kernel,
        out_shape=(
            jax.ShapeDtypeStruct((D // HEADS, SPAN, TILE), BF16),
            token, token, token,
            jax.ShapeDtypeStruct((D // GROUP, HD), F32),
        ),
        in_specs=[any_spec] * 6,
        out_specs=(any_spec,) * 5,
        scratch_shapes=[
            vmem((D // HEADS, SPAN, TILE), BF16),
            vmem((D // HEADS, TOKENS), F32),
            vmem((TOKENS, HD), BF16),
            vmem((TOKENS, HD), BF16),
            vmem((TOKENS, HD), BF16),
            vmem((D // GROUP, HD), F32),
            vmem((NT, NH, SPAN, TILE), jnp.int32),
            vmem((TOKENS, HD), BF16),
            vmem((SLOTS, 2) + unit, BF16),
            vmem((SLOTS, HD, TOKENS), BF16),
            vmem((SLOTS, HD, TOKENS), BF16),
            vmem((TOKENS, HD), BF16),
            vmem((D, HD), BF16),
            vmem((D, SPAN, TILE), BF16),
            vmem((D, TOKENS), BF16),
            vmem((SPAN, 2 * HD, TILE), BF16),
            vmem((TOKENS, HD), BF16),
            vmem((SPAN, 2 * HD, TILE), BF16),
            vmem((SLOTS, len(PAIRS), TILE, TILE), BF16),
            vmem((len(PAIRS), TILE, TILE), BF16),
            vmem((len(PAIRS), TILE, TILE), BF16),
            vmem((SPAN, HD + 16, TILE), F32),
            vmem((SPAN, 1, TILE), F32),
            vmem((SLOTS, 2, SPAN, 1, TILE), F32),
            vmem((SPAN, 1, TILE), F32),
            vmem((SPAN, HD, TILE), F32),
            vmem((2,) + unit, F32),
            vmem((SLOTS, 2) + unit, BF16),
            vmem((3, 2) + unit, BF16),
            vmem((2, 2) + unit, BF16),
            vmem((2,) + unit, BF16),
            vmem((2, HALF, HD), BF16),
            vmem((2, HALF, HD), BF16),
            vmem((2,) + unit, BF16),
            vmem((HEADS, HD, TOKENS), BF16),
            vmem((2, HEADS, D // HEADS // 2, HD), BF16),
            vmem((2,) + pieces, BF16),
            vmem(pieces, BF16),
            vmem(pieces, BF16),
            vmem(pieces, BF16),
            dma((8,)), dma((5,)), dma((10, 2)), dma((SLOTS, 2)), dma((18,)), dma((18,)),
            dma((9,)), dma((9,)), dma((HEADS,)), dma((HEADS,)), dma((GROUP // 2,)), dma((GROUP // 2,)),
        ],
        compiler_params=pltpu.CompilerParams(
            collective_id=0, has_side_effects=True, vmem_limit_bytes=60 * 1024 * 1024
        ),
    )(
        queries.reshape(TOKENS, HD),
        key_tiles.reshape(TOKENS, HD),
        values.reshape(TOKENS, HD),
        token_valid,
        out_weight,
        out_grad.reshape(D, SPAN, TILE),
    )
    mixed, dq, dk, dv, wg = pl.pallas_call(
        hand_over,
        out_shape=[jax.ShapeDtypeStruct(r.shape, r.dtype) for r in results],
        in_specs=[any_spec] * 5,
        out_specs=[any_spec] * 5,
        scratch_shapes=[vmem(r.shape, r.dtype) for r in results] + [dma((10,))],
    )(*results)
    tile_shape = (1, 1, 1, SPAN, TILE, HD)
    return (
        mixed.reshape(D // HEADS, 1, 1, SPAN, TILE),
        dq.reshape(tile_shape),
        dk.reshape(tile_shape),
        dv.reshape(tile_shape),
        wg,
    )


def solution(mesh):
    placed = (
        P("head", "tm", "height", None, None, None),
        P("head", "tm", "height", None, None, None),
        P("head", "tm", "height", None, None, None),
        P(),
        P(None, "head"),
        P(None, "tm", "height", None, None),
    )
    return jax.shard_map(
        per_device,
        mesh=mesh,
        in_specs=placed,
        out_specs=(
            P("head", "tm", "height", None, None),
            P("head", "tm", "height", None, None, None),
            P("head", "tm", "height", None, None, None),
            P("head", "tm", "height", None, None, None),
            P(("tm", "height"), "head"),
        ),
        check_vma=False,
    )
```

```python
import functools
import math

import jax
import jax.numpy as jnp
from jax import lax
from jax.experimental import pallas as pl
from jax.experimental.pallas import tpu as pltpu
from jax.sharding import PartitionSpec as P

MESH = pl.DeviceIdType.MESH
F32 = jnp.float32
BF16 = jnp.bfloat16

TILE = 256
SPAN = 4
TOKENS = TILE * SPAN
HD = 128
D = 1536
HEADS = 8
NT = 4
NH = 4
GROUP = NT * NH
SCALE = 1.0 / math.sqrt(HD)
EXPO = SCALE * math.log2(math.e)
LOWEST = -1e30

SLOTS = 9
HALF = TOKENS // 2
LAST_ORDER = (2, 3, 4, 1, 0)

PAIRS = [(k, q) for k in range(SPAN) for q in range(SPAN) if abs(k - q) <= 1]
PAIR_AT = {pair: i for i, pair in enumerate(PAIRS)}


def dot(lhs, rhs, dims=((1,), (0,))):
    return lax.dot_general(lhs, rhs, (dims, ((), ())), preferred_element_type=F32)


def chosen(index, table):
    value = jnp.int32(table[0])
    for at, entry in enumerate(table):
        value = jnp.where(index == at, jnp.int32(entry), value)
    return value


def kernel(
    q_ref, k_ref, v_ref, tv_ref, w_ref, og_ref,
    mixed_ref, dq_ref, dk_ref, dv_ref, wg_ref,
    mixed_s, most_s, dq_s, dk_s, dv_s, wg_s, tv_s,
    q_s, kv_s, kt_s, vt_s, mask_s, w_s, raw_s, og_s,
    qt_s, do_s, dot_s, p_s, ps_s, ds_s, att_s, m_s, mb_s, rl_s, dqt_s,
    acc_s, send_s, rp_s, rz_s, rx_s, rd_s, rw_s, ry_s, ag_s, wgat_s, prod_s, pair_s, sum_s, red_s,
    loc_sem, f_send, f_recv, b_recv, ag_send, ag_recv, wt_send, wt_recv, pr_send, pr_recv,
):
    a = lax.axis_index("tm")
    b = lax.axis_index("height")
    h = lax.axis_index("head")
    inner = jnp.logical_or(a == 1, a == 2)
    has_lo = b > 0
    has_hi = b < NH - 1
    partner = a + 1 - 2 * (a % 2)
    cross = NT - 1 - a
    here = a * NH + b
    dev_partner = (partner, b, h)
    dev_cross = (cross, b, h)
    dev_lo = (a, b - 1, h)
    dev_hi = (a, b + 1, h)
    both = jnp.logical_and

    loads = [
        pltpu.make_async_copy(src, dst, loc_sem.at[i])
        for i, (src, dst) in enumerate([(q_ref, q_s), (tv_ref, tv_s), (w_ref, w_s), (og_ref, raw_s)])
    ]
    for part in range(2):
        for kind, ref in enumerate((k_ref, v_ref)):
            pltpu.make_async_copy(
                ref.at[pl.ds(part * HALF, HALF)], kv_s.at[0, part, kind], loc_sem.at[4]
            ).start()
    for load in loads:
        load.start()

    barrier = pltpu.get_barrier_semaphore()
    for j in range(1, GROUP):
        peer = (here + j) % GROUP
        pl.semaphore_signal(barrier, inc=1, device_id=(peer // NH, peer % NH, h), device_id_type=MESH)
    for j in range(1, HEADS):
        pl.semaphore_signal(barrier, inc=1, device_id=(a, b, (h + j) % HEADS), device_id_type=MESH)
    pl.semaphore_wait(barrier, GROUP - 1 + HEADS - 1)

    def remote(src, dst, send, recv, device):
        return pltpu.make_async_remote_copy(
            src_ref=src, dst_ref=dst, send_sem=send, recv_sem=recv, device_id=device, device_id_type=MESH
        )

    yes = a >= 0
    hops = [
        (0, 3, dev_hi, has_hi, (0, 1)),
        (0, 4, dev_lo, has_lo, (0, 1)),
        (0, 2, dev_cross, inner, (0, 1)),
        (0, 1, dev_partner, yes, (0, 1)),
        (3, 5, dev_partner, has_lo, (0, 1)),
        (4, 6, dev_partner, has_hi, (0, 1)),
        (2, 7, dev_hi, both(inner, has_hi), (1,)),
        (2, 8, dev_lo, both(inner, has_lo), (1,)),
        (3, 7, dev_cross, both(inner, has_lo), (0,)),
        (4, 8, dev_cross, both(inner, has_hi), (0,)),
    ]
    arrives = [yes, yes, inner, has_lo, has_hi, has_lo, has_hi, both(inner, has_lo), both(inner, has_hi)]

    def hop_copy(n, part):
        source, target, device, _, _ = hops[n]
        return remote(
            kv_s.at[source, part], kv_s.at[target, part], f_send.at[n, part], f_recv.at[target, part], device
        )

    def start_hop(n, part):
        @pl.when(hops[n][3])
        def _():
            hop_copy(n, part).start()

    def wait_unit(slot, part):
        @pl.when(arrives[slot])
        def _():
            remote(
                kv_s.at[slot, part], kv_s.at[slot, part], f_send.at[0, 0], f_recv.at[slot, part], dev_partner
            ).wait_recv()

    pltpu.make_async_copy(kv_s.at[0], kv_s.at[0], loc_sem.at[4]).wait()
    for part in range(2):
        for n in range(4):
            start_hop(n, part)

    share = D // HEADS

    part_share = share // 2
    core = a % 2

    def weight_rows(peer):
        return pl.ds(pl.multiple_of(peer * share + core * part_share, part_share), part_share)

    def weight_copy(j):
        peer = (h + j) % HEADS
        return remote(
            w_ref.at[weight_rows(peer)], wgat_s.at[core, h], wt_send.at[0], wt_recv.at[0], (a, b, peer)
        )

    def weight_exchange():
        return remote(wgat_s.at[core], wgat_s.at[core], wt_send.at[1], wt_recv.at[1], dev_partner)

    def weight_copies():
        others = wgat_s.at[core, pl.ds(0, HEADS - 1)]
        return remote(others, others, wt_send.at[0], wt_recv.at[0], dev_partner)

    for j in range(1, HEADS):
        weight_copy(j).start()

    loads[0].wait()
    loads[1].wait()
    first_row = (lax.broadcasted_iota(jnp.int32, (HD, TILE), 0) == 0).astype(BF16)
    for c in range(SPAN):
        rows = slice(c * TILE, (c + 1) * TILE)
        qt_s[c, :HD] = q_s[rows].T
        qt_s[c, HD:] = first_row
        m_s[c] = jnp.full((1, TILE), LOWEST, F32)
        att_s[c] = jnp.zeros((HD + 16, TILE), F32)
    ones_rows = jnp.ones((16, TOKENS), BF16)
    ones_cols = jnp.ones((TILE, HD), BF16)

    def keys_of(c, tiles):
        near = [t for t in tiles if abs(t - c) <= 1]
        return (near[0], near[-1] + 1) if near else (0, 0)

    def tile_of(ref, slot, kind, t):
        return ref[slot, t // 2, kind, (t % 2) * TILE:(t % 2 + 1) * TILE]

    def queries_of(t):
        return max(0, t - 1), min(SPAN, t + 2)

    def near_queries(tiles):
        return [c for c in range(SPAN) if keys_of(c, tiles)[1]]

    def place(slot):
        frame = chosen(slot, (0, 1, 2, 0, 0, 1, 1, 2, 2))
        frame = jnp.where(frame == 0, a, jnp.where(frame == 1, partner, cross))
        row = b + chosen(slot, (0, 0, 0, -1, 1, -1, 1, -1, 1))
        return frame, row

    def exists(slot):
        far = chosen(slot, (0, 0, 1, 0, 0, 0, 0, 1, 1))
        row = b + chosen(slot, (0, 0, 0, -1, 1, -1, 1, -1, 1))
        near = both(row >= 0, row < NH)
        return both(near, jnp.logical_or(far == 0, inner))

    def forward_unit(slot, tiles):
        frame, row = place(slot)
        for t in tiles:
            rows = slice(t * TILE, (t + 1) * TILE)
            kt_s[slot, :, rows] = tile_of(kv_s, slot, 0, t).T
            vt_s[slot, :, rows] = tile_of(kv_s, slot, 1, t).T
            valid = tv_s[frame, row, t:t + 1, :]
            bias = jnp.where(valid > 0, 0.0, LOWEST)
            mask_s[rows] = jnp.broadcast_to(bias, (HD, TILE)).T.astype(BF16)
        shrink = {}
        for c in near_queries(tiles):
            lo, hi = keys_of(c, tiles)
            keys = jnp.concatenate([tile_of(kv_s, slot, 0, t) for t in range(lo, hi)], axis=0)
            keys = jnp.concatenate([keys, mask_s[lo * TILE:hi * TILE]], axis=1)
            scores = dot(keys, qt_s[c])
            old = m_s[c]
            new = jnp.maximum(old, jnp.max(scores, axis=0, keepdims=True))
            weights = jnp.exp2((scores - new) * EXPO).astype(BF16)
            for t in range(lo, hi):
                p_s[slot, PAIR_AT[t, c]] = weights[(t - lo) * TILE:(t - lo + 1) * TILE]
            shrink[c] = jnp.exp2((old - new) * EXPO)
            m_s[c] = new
            for part in sorted({t // 2 for t in range(lo, hi)}):
                mb_s[slot, part, c] = new
        for c in near_queries(tiles):
            lo, hi = keys_of(c, tiles)
            rows = slice(lo * TILE, hi * TILE)
            vals = jnp.concatenate([vt_s[slot, :, rows], ones_rows[:, rows]], axis=0)
            weights = jnp.concatenate([p_s[slot, PAIR_AT[t, c]] for t in range(lo, hi)], axis=0)
            att_s[c] = att_s[c] * shrink[c] + dot(vals, weights)

    def grad_attended():
        for load in loads[2:]:
            load.wait()
        for n in range(0, D, HD):
            og_s[n:n + HD] = raw_s[n:n + HD].reshape(HD, TOKENS)
        for c in range(SPAN):
            rows = slice(c * TILE, (c + 1) * TILE)
            grad = dot(w_s[...], og_s[:, rows], ((0,), (0,))).astype(BF16)
            dot_s[c, :HD] = grad
            do_s[rows] = grad.T

    every = tuple(range(SPAN))

    def forward_pass(first, count, tiles, events):
        def step(i, carry):
            for at, waits in events.items():
                @pl.when(i == at - first)
                def _():
                    if at == 1:
                        grad_attended()
                    for source, part, starts in waits:
                        wait_unit(source, part)
                        for n in starts:
                            start_hop(n, part)

            @pl.when(exists(i + first))
            def _():
                forward_unit(i + first, tiles)

            return carry

        lax.fori_loop(0, count, step, 0)

    forward_pass(0, 2, every, {1: [(1, 0, ()), (1, 1, ())]})
    forward_pass(2, 5, (0, 1), {
        2: [(2, 0, ())],
        3: [(3, 0, (4, 8)), (4, 0, (5, 9))],
        5: [(2, 1, (6, 7)), (5, 0, ())],
        6: [(6, 0, ())],
    })
    forward_pass(2, 5, (2, 3), {3: [(3, 1, (4,)), (4, 1, (5,))], 5: [(5, 1, ())], 6: [(6, 1, ())]})
    forward_pass(7, 2, every, {7: [(7, 0, ()), (7, 1, ())], 8: [(8, 0, ()), (8, 1, ())]})

    for c in range(SPAN):
        rows = slice(c * TILE, (c + 1) * TILE)
        inverse = 1.0 / att_s[c, HD:HD + 1]
        rl_s[c] = inverse
        attended = (att_s[c, :HD] * inverse).astype(BF16)
        ag_s[h, :, rows] = attended
        delta = jnp.sum(dot_s[c, :HD].astype(F32) * attended.astype(F32), axis=0, keepdims=True)
        high = delta.astype(BF16).astype(F32)
        middle = (delta - high).astype(BF16).astype(F32)
        low = delta - high - middle
        index = lax.broadcasted_iota(jnp.int32, (HD, TILE), 0)
        extra = jnp.where(index == 0, -high, jnp.where(index == 1, -middle, jnp.where(index == 2, -low, 0.0)))
        dot_s[c, HD:] = extra.astype(BF16)
        dqt_s[c] = jnp.zeros((HD, TILE), F32)

    side = h + 1 - 2 * (h % 2)
    up, down = (h + 2) % HEADS, (h + HEADS - 2) % HEADS
    side_up, side_down = (side + 2) % HEADS, (side + HEADS - 2) % HEADS
    half = HD // 2
    low_half, high_half = pl.ds(0, half), pl.ds(half, half)
    gathers = [
        (ag_s.at[h], side),
        (ag_s.at[h], up),
        (ag_s.at[h], down),
        (ag_s.at[side], up),
        (ag_s.at[side], down),
        (ag_s.at[down, low_half], up),
        (ag_s.at[up, high_half], down),
        (ag_s.at[side_down, low_half], up),
        (ag_s.at[side_up, high_half], down),
    ]

    def gather_copy(n):
        block, peer = gathers[n]
        return remote(block, block, ag_send.at[n], ag_recv.at[n], (a, b, peer))

    def relay(waits, starts):
        for n in waits:
            gather_copy(n).wait_recv()
        for n in starts:
            gather_copy(n).start()

    relay((), (0, 1, 2))

    piece = D // GROUP
    chips = GROUP // 2
    chip = (a // 2) * NH + b

    def pair_copy():
        return remote(prod_s.at[1 - core], pair_s, pr_send.at[0], pr_recv.at[0], dev_partner)

    def part_copy(j):
        peer = (chip + j) % chips
        return remote(
            sum_s.at[peer], red_s.at[chip], pr_send.at[1], pr_recv.at[1], ((peer // NH) * 2 + core, peer % NH, h)
        )

    def part_copies():
        others = red_s.at[pl.ds(0, chips - 1)]
        return remote(others, others, pr_send.at[1], pr_recv.at[1], dev_partner)

    def weight_product():
        for frame in range(NT):
            first = frame * NH * piece
            value = dot(og_s[first:first + NH * piece], ag_s[h], ((1,), (1,))).astype(BF16)
            for row in range(NH):
                prod_s[frame % 2, (frame // 2) * NH + row] = value[row * piece:(row + 1) * piece]
        pair_copy().start()

    def weight_parts():
        pair_copy().wait_recv()
        sum_s[...] = (prod_s[core].astype(F32) + pair_s[...].astype(F32)).astype(BF16)
        for j in range(1, chips):
            part_copy(j).start()

    for n in range(len(hops)):
        @pl.when(hops[n][3])
        def _():
            for part in hops[n][4]:
                hop_copy(n, part).wait_send()

    weight_product()

    def backward_unit(slot, tiles):
        factors = {
            (part, c): jnp.exp2((mb_s[slot, part, c] - m_s[c]) * EXPO) * rl_s[c]
            for part in sorted({t // 2 for t in tiles}) for c in near_queries((2 * part, 2 * part + 1))
        }
        for t in tiles:
            vals = jnp.concatenate([tile_of(kv_s, slot, 1, t), ones_cols], axis=1)
            for c in range(*queries_of(t)):
                n = PAIR_AT[t, c]
                grad = dot(vals, dot_s[c])
                probs = p_s[slot, n].astype(F32) * factors[t // 2, c]
                ps_s[n] = probs.astype(BF16)
                ds_s[n] = (probs * grad).astype(BF16)
        for t in tiles:
            rows = slice((t % 2) * TILE, (t % 2 + 1) * TILE)
            lo, hi = queries_of(t)
            near = slice(lo * TILE, hi * TILE)
            many_ds = jnp.concatenate([ds_s[PAIR_AT[t, c]] for c in range(lo, hi)], axis=1)
            many_ps = jnp.concatenate([ps_s[PAIR_AT[t, c]] for c in range(lo, hi)], axis=1)
            send_s[slot, t // 2, 0, rows] = (dot(many_ds, q_s[near]) * SCALE).astype(BF16)
            send_s[slot, t // 2, 1, rows] = dot(many_ps, do_s[near]).astype(BF16)
        for c in near_queries(tiles):
            lo, hi = keys_of(c, tiles)
            many = jnp.concatenate([ds_s[PAIR_AT[t, c]] for t in range(lo, hi)], axis=0)
            dqt_s[c] += dot(kt_s[slot, :, lo * TILE:hi * TILE], many)

    back = {
        (7, 0): (rd_s.at[0], 0, dev_cross, both(inner, has_lo), both(inner, has_lo)),
        (8, 0): (rd_s.at[1], 1, dev_cross, both(inner, has_hi), both(inner, has_hi)),
        (7, 1): (rx_s.at[0], 2, dev_lo, both(inner, has_lo), both(inner, has_hi)),
        (8, 1): (rx_s.at[1], 3, dev_hi, both(inner, has_hi), both(inner, has_lo)),
        (7, 2): (rw_s.at[0], 16, dev_lo, both(inner, has_lo), both(inner, has_hi)),
        (8, 2): (rw_s.at[1], 17, dev_hi, both(inner, has_hi), both(inner, has_lo)),
    }
    inside = {0: (0, 0), 2: (0, 1)}

    for part in range(2):
        at = 4 + 6 * part
        back[5, part] = (rp_s.at[1, part], at, dev_partner, has_lo, has_lo)
        back[6, part] = (rp_s.at[2, part], at + 1, dev_partner, has_hi, has_hi)
        back[3, part] = (rz_s.at[0, part], at + 2, dev_lo, has_lo, has_hi)
        back[4, part] = (rz_s.at[1, part], at + 3, dev_hi, has_hi, has_lo)
        back[2, part] = (ry_s.at[part], at + 4, dev_cross, inner, inner)
        back[1, part] = (rp_s.at[0, part], at + 5, dev_partner, yes, yes)
    needs = {key: () for key in back}
    needs[3, 0], needs[4, 0] = ((5, 0), (7, 0)), ((6, 0), (8, 0))
    needs[3, 1], needs[4, 1] = ((5, 1),), ((6, 1),)
    needs[2, 0] = ((7, 2), (8, 2))
    needs[2, 1] = ((7, 1), (8, 1))

    def back_copy(key):
        slot, part = key
        target, index, device, _, _ = back[key]
        source = send_s.at[(slot,) + inside[part]] if slot > 6 and part in inside else send_s.at[slot, part]
        return remote(source, target, f_send.at[index // 2, index % 2], b_recv.at[index], device)

    def merge(key, source):
        @pl.when(back[source][4])
        def _():
            back_copy(source).wait_recv()
            at = (key[0],) + inside[source[1]] if source[0] > 6 and source[1] in inside else key
            arrived = back[source][0][...].astype(F32)
            send_s[at] = (send_s[at].astype(F32) + arrived).astype(BF16)

    def give_back(key, who):
        @pl.when(both(who, back[key][3]))
        def _():
            for source in needs[key]:
                merge(key, source)
            back_copy(key).start()

    outer = jnp.logical_not(inner)

    def first_step(i, carry):
        slot = jnp.where(inner, 7 + i, 3 + i)

        @pl.when(i == 1)
        def _():
            weight_parts()

        @pl.when(exists(slot))
        def _():
            backward_unit(slot, every)

        for n in (7, 8):
            @pl.when(i == n - 7)
            def _():
                for part in range(3):
                    give_back((n, part), inner)

        return carry

    lax.fori_loop(0, 2, first_step, 0)

    for part in range(2):
        def partner_step(i, carry):
            if part == 1:
                @pl.when(i == 1)
                def _():
                    relay((0,), (3, 4))

            @pl.when(exists(i + 5))
            def _():
                backward_unit(i + 5, (2 * part, 2 * part + 1))

            for n in (5, 6):
                @pl.when(i == n - 5)
                def _():
                    give_back((n, part), yes)

            return carry

        lax.fori_loop(0, 2, partner_step, 0)
        for n in (3, 4):
            give_back((n, part), outer)

    def last_step(i, carry):
        slot = chosen(i, LAST_ORDER)
        own_side = both(slot >= 3, outer)

        @pl.when(i == 0)
        def _():
            relay((1, 2), (5, 6))

        @pl.when(i == 3)
        def _():
            wgat_s[core, h] = w_s[weight_rows(h)]
            weight_copies().wait_recv()
            weight_exchange().start()

            @pl.when(inner)
            def _():
                relay((3, 4), (7, 8))

        @pl.when(i == 4)
        def _():
            @pl.when(outer)
            def _():
                relay((3, 4), (7, 8))

        @pl.when(both(exists(slot), jnp.logical_not(own_side)))
        def _():
            backward_unit(slot, every)

        for n in range(1, 5):
            @pl.when(slot == n)
            def _():
                for part in range(2):
                    give_back((n, part), inner if n in (3, 4) else yes)

        return carry

    lax.fori_loop(0, len(LAST_ORDER), last_step, 0)

    for c in range(SPAN):
        rows = slice(c * TILE, (c + 1) * TILE)
        dq_s[rows] = (dqt_s[c] * SCALE).T.astype(BF16)

    stores = [
        pltpu.make_async_copy(src, dst, loc_sem.at[i])
        for i, (src, dst) in enumerate(
            [(mixed_s, mixed_ref), (dq_s, dq_ref), (dk_s, dk_ref), (dv_s, dv_ref), (wg_s, wg_ref)]
        )
    ]
    stores[1].start()

    def projected(heads):
        rows = [jnp.concatenate([wgat_s[i, n] for n in heads], axis=1) for i in range(2)]
        return dot(jnp.concatenate(rows, axis=0), jnp.concatenate([ag_s[n] for n in heads], axis=0))

    weight_exchange().wait_recv()
    most_s[...] = projected((h, side, up, down, side_up, side_down))
    for part in range(2):
        back_copy((1, part)).wait_recv()
        acc_s[part] = send_s[0, part].astype(F32) + rp_s[0, part].astype(F32)
    for part in range(2):
        for source in (4, 3, 2):
            @pl.when(back[source, part][4])
            def _():
                back_copy((source, part)).wait_recv()
                acc_s[part] += back[source, part][0][...].astype(F32)
        rows = slice(part * HALF, (part + 1) * HALF)
        dk_s[rows] = acc_s[part, 0].astype(BF16)
        dv_s[rows] = acc_s[part, 1].astype(BF16)

    stores[2].start()
    stores[3].start()

    relay((5, 6, 7, 8), ())
    far = (h + HEADS // 2) % HEADS
    mixed = most_s[...] + projected((far, (side + HEADS // 2) % HEADS))
    mixed_s[...] = mixed.astype(BF16).reshape(share, SPAN, TILE)
    stores[0].start()

    red_s[chip] = sum_s[chip]
    part_copies().wait_recv()
    total = red_s[0].astype(F32)
    for n in range(1, chips):
        total = total + red_s[n].astype(F32)
    wg_s[...] = total
    stores[4].start()

    for key, (_, _, _, sends, _) in back.items():
        @pl.when(sends)
        def _():
            back_copy(key).wait_send()
    weight_exchange().wait_send()
    weight_copies().wait_send()
    for n in range(len(gathers)):
        gather_copy(n).wait_send()
    pair_copy().wait_send()
    part_copies().wait_send()
    for store in stores:
        store.wait()


def hand_over(*refs):
    sources, targets, staged, sem = refs[:5], refs[5:10], refs[10:15], refs[15]
    reads = [pltpu.make_async_copy(sources[i], staged[i], sem.at[i]) for i in range(5)]
    writes = [pltpu.make_async_copy(staged[i], targets[i], sem.at[i]) for i in range(5)]
    for read in reads:
        read.start()
    for read, write in zip(reads, writes):
        read.wait()
        write.start()
    for write in writes:
        write.wait()


def per_device(queries, key_tiles, values, token_valid, out_weight, out_grad):
    any_spec = pl.BlockSpec(memory_space=pl.ANY)
    vmem = pltpu.VMEM
    dma = pltpu.SemaphoreType.DMA
    token = jax.ShapeDtypeStruct((TOKENS, HD), BF16)
    unit = (2, HALF, HD)
    pieces = (GROUP // 2, D // GROUP, HD)
    results = pl.pallas_call(
        kernel,
        out_shape=(
            jax.ShapeDtypeStruct((D // HEADS, SPAN, TILE), BF16),
            token, token, token,
            jax.ShapeDtypeStruct((D // GROUP, HD), F32),
        ),
        in_specs=[any_spec] * 6,
        out_specs=(any_spec,) * 5,
        scratch_shapes=[
            vmem((D // HEADS, SPAN, TILE), BF16),
            vmem((D // HEADS, TOKENS), F32),
            vmem((TOKENS, HD), BF16),
            vmem((TOKENS, HD), BF16),
            vmem((TOKENS, HD), BF16),
            vmem((D // GROUP, HD), F32),
            vmem((NT, NH, SPAN, TILE), jnp.int32),
            vmem((TOKENS, HD), BF16),
            vmem((SLOTS, 2) + unit, BF16),
            vmem((SLOTS, HD, TOKENS), BF16),
            vmem((SLOTS, HD, TOKENS), BF16),
            vmem((TOKENS, HD), BF16),
            vmem((D, HD), BF16),
            vmem((D, SPAN, TILE), BF16),
            vmem((D, TOKENS), BF16),
            vmem((SPAN, 2 * HD, TILE), BF16),
            vmem((TOKENS, HD), BF16),
            vmem((SPAN, 2 * HD, TILE), BF16),
            vmem((SLOTS, len(PAIRS), TILE, TILE), BF16),
            vmem((len(PAIRS), TILE, TILE), BF16),
            vmem((len(PAIRS), TILE, TILE), BF16),
            vmem((SPAN, HD + 16, TILE), F32),
            vmem((SPAN, 1, TILE), F32),
            vmem((SLOTS, 2, SPAN, 1, TILE), F32),
            vmem((SPAN, 1, TILE), F32),
            vmem((SPAN, HD, TILE), F32),
            vmem((2,) + unit, F32),
            vmem((SLOTS, 2) + unit, BF16),
            vmem((3, 2) + unit, BF16),
            vmem((2, 2) + unit, BF16),
            vmem((2,) + unit, BF16),
            vmem((2, HALF, HD), BF16),
            vmem((2, HALF, HD), BF16),
            vmem((2,) + unit, BF16),
            vmem((HEADS, HD, TOKENS), BF16),
            vmem((2, HEADS, D // HEADS // 2, HD), BF16),
            vmem((2,) + pieces, BF16),
            vmem(pieces, BF16),
            vmem(pieces, BF16),
            vmem(pieces, BF16),
            dma((5,)), dma((10, 2)), dma((SLOTS, 2)), dma((18,)),
            dma((9,)), dma((9,)), dma((2,)), dma((2,)), dma((2,)), dma((2,)),
        ],
        compiler_params=pltpu.CompilerParams(
            collective_id=0, has_side_effects=True, vmem_limit_bytes=60 * 1024 * 1024
        ),
    )(
        queries.reshape(TOKENS, HD),
        key_tiles.reshape(TOKENS, HD),
        values.reshape(TOKENS, HD),
        token_valid,
        out_weight,
        out_grad.reshape(D, SPAN, TILE),
    )
    mixed, dq, dk, dv, wg = pl.pallas_call(
        hand_over,
        out_shape=[jax.ShapeDtypeStruct(r.shape, r.dtype) for r in results],
        in_specs=[any_spec] * 5,
        out_specs=[any_spec] * 5,
        scratch_shapes=[vmem(r.shape, r.dtype) for r in results] + [dma((5,))],
    )(*results)
    tile_shape = (1, 1, 1, SPAN, TILE, HD)
    return (
        mixed.reshape(D // HEADS, 1, 1, SPAN, TILE),
        dq.reshape(tile_shape),
        dk.reshape(tile_shape),
        dv.reshape(tile_shape),
        wg,
    )


def solution(mesh):
    placed = (
        P("head", "tm", "height", None, None, None),
        P("head", "tm", "height", None, None, None),
        P("head", "tm", "height", None, None, None),
        P(),
        P(None, "head"),
        P(None, "tm", "height", None, None),
    )
    return jax.shard_map(
        per_device,
        mesh=mesh,
        in_specs=placed,
        out_specs=(
            P("head", "tm", "height", None, None),
            P("head", "tm", "height", None, None, None),
            P("head", "tm", "height", None, None, None),
            P("head", "tm", "height", None, None, None),
            P(("tm", "height"), "head"),
        ),
        check_vma=False,
    )
```

```python
import functools
import math

import jax
import jax.numpy as jnp
from jax import lax
from jax.experimental import pallas as pl
from jax.experimental.pallas import tpu as pltpu
from jax.sharding import PartitionSpec as P

MESH = pl.DeviceIdType.MESH
F32 = jnp.float32
BF16 = jnp.bfloat16

TILE = 256
SPAN = 4
TOKENS = TILE * SPAN
HD = 128
D = 1536
HEADS = 8
NT = 4
NH = 4
GROUP = NT * NH
SCALE = 1.0 / math.sqrt(HD)
EXPO = SCALE * math.log2(math.e)
LOWEST = -1e30

SLOTS = 9
HALF = TOKENS // 2
LAST_ORDER = (3, 2, 4, 1, 0)

PAIRS = [(k, q) for k in range(SPAN) for q in range(SPAN) if abs(k - q) <= 1]
PAIR_AT = {pair: i for i, pair in enumerate(PAIRS)}


def dot(lhs, rhs, dims=((1,), (0,))):
    return lax.dot_general(lhs, rhs, (dims, ((), ())), preferred_element_type=F32)


def chosen(index, table):
    value = jnp.int32(table[0])
    for at, entry in enumerate(table):
        value = jnp.where(index == at, jnp.int32(entry), value)
    return value


def kernel(
    q_ref, k_ref, v_ref, tv_ref, w_ref, og_ref,
    mixed_ref, dq_ref, dk_ref, dv_ref, wg_ref,
    mixed_s, most_s, dq_s, dk_s, dv_s, wg_s, tv_s,
    q_s, kv_s, kt_s, vt_s, mask_s, w_s, raw_s, og_s,
    qt_s, do_s, dot_s, p_s, ps_s, ds_s, att_s, m_s, mb_s, rl_s, dqt_s,
    acc_s, send_s, rp_s, rz_s, rx_s, rd_s, rw_s, ry_s, ag_s, wgat_s, prod_s, pair_s, sum_s, red_s,
    loc_sem, f_send, f_recv, b_recv, ag_send, ag_recv, wt_send, wt_recv, pr_send, pr_recv,
):
    a = lax.axis_index("tm")
    b = lax.axis_index("height")
    h = lax.axis_index("head")
    inner = jnp.logical_or(a == 1, a == 2)
    outer = jnp.logical_not(inner)
    has_lo = b > 0
    has_hi = b < NH - 1
    partner = a + 1 - 2 * (a % 2)
    cross = NT - 1 - a
    here = a * NH + b
    dev_partner = (partner, b, h)
    dev_cross = (cross, b, h)
    dev_lo = (a, b - 1, h)
    dev_hi = (a, b + 1, h)
    both = jnp.logical_and

    loads = [
        pltpu.make_async_copy(src, dst, loc_sem.at[i])
        for i, (src, dst) in enumerate([(q_ref, q_s), (tv_ref, tv_s), (w_ref, w_s), (og_ref, raw_s)])
    ]
    for part in range(2):
        for kind, ref in enumerate((k_ref, v_ref)):
            pltpu.make_async_copy(
                ref.at[pl.ds(part * HALF, HALF)], kv_s.at[0, part, kind], loc_sem.at[4]
            ).start()
    for load in loads:
        load.start()

    barrier = pltpu.get_barrier_semaphore()
    for j in range(1, GROUP):
        peer = (here + j) % GROUP
        pl.semaphore_signal(barrier, inc=1, device_id=(peer // NH, peer % NH, h), device_id_type=MESH)
    for j in range(1, HEADS):
        pl.semaphore_signal(barrier, inc=1, device_id=(a, b, (h + j) % HEADS), device_id_type=MESH)
    pl.semaphore_wait(barrier, GROUP - 1 + HEADS - 1)

    def remote(src, dst, send, recv, device):
        return pltpu.make_async_remote_copy(
            src_ref=src, dst_ref=dst, send_sem=send, recv_sem=recv, device_id=device, device_id_type=MESH
        )

    yes = a >= 0
    hops = [
        (0, 3, dev_hi, has_hi, (0, 1)),
        (0, 4, dev_lo, has_lo, (0, 1)),
        (0, 2, dev_cross, inner, (0, 1)),
        (0, 1, dev_partner, yes, (0, 1)),
        (3, 5, dev_partner, has_lo, (0, 1)),
        (4, 6, dev_partner, has_hi, (0, 1)),
        (2, 7, dev_hi, both(inner, has_hi), (1,)),
        (2, 8, dev_lo, both(inner, has_lo), (1,)),
        (3, 7, dev_cross, both(inner, has_lo), (0,)),
        (4, 8, dev_cross, both(inner, has_hi), (0,)),
    ]
    arrives = [yes, yes, inner, has_lo, has_hi, has_lo, has_hi, both(inner, has_lo), both(inner, has_hi)]

    def hop_copy(n, part):
        source, target, device, _, _ = hops[n]
        return remote(
            kv_s.at[source, part], kv_s.at[target, part], f_send.at[n, part], f_recv.at[target, part], device
        )

    def start_hop(n, part):
        @pl.when(hops[n][3])
        def _():
            hop_copy(n, part).start()

    def wait_unit(slot, part):
        @pl.when(arrives[slot])
        def _():
            remote(
                kv_s.at[slot, part], kv_s.at[slot, part], f_send.at[0, 0], f_recv.at[slot, part], dev_partner
            ).wait_recv()

    pltpu.make_async_copy(kv_s.at[0], kv_s.at[0], loc_sem.at[4]).wait()
    for part in range(2):
        for n in range(4):
            start_hop(n, part)

    share = D // HEADS

    part_share = share // 2
    core = a % 2

    def weight_rows(peer):
        return pl.ds(pl.multiple_of(peer * share + core * part_share, part_share), part_share)

    def weight_copy(j):
        peer = (h + j) % HEADS
        return remote(
            w_ref.at[weight_rows(peer)], wgat_s.at[core, h], wt_send.at[0], wt_recv.at[0], (a, b, peer)
        )

    def weight_exchange():
        return remote(wgat_s.at[core], wgat_s.at[core], wt_send.at[1], wt_recv.at[1], dev_partner)

    def weight_copies():
        others = wgat_s.at[core, pl.ds(0, HEADS - 1)]
        return remote(others, others, wt_send.at[0], wt_recv.at[0], dev_partner)

    for j in range(1, HEADS):
        weight_copy(j).start()

    loads[0].wait()
    loads[1].wait()
    first_row = (lax.broadcasted_iota(jnp.int32, (HD, TILE), 0) == 0).astype(BF16)
    for c in range(SPAN):
        rows = slice(c * TILE, (c + 1) * TILE)
        qt_s[c, :HD] = q_s[rows].T
        qt_s[c, HD:] = first_row
        m_s[c] = jnp.full((1, TILE), LOWEST, F32)
        att_s[c] = jnp.zeros((HD + 16, TILE), F32)
    ones_rows = jnp.ones((16, TOKENS), BF16)
    ones_cols = jnp.ones((TILE, HD), BF16)

    def keys_of(c, tiles):
        near = [t for t in tiles if abs(t - c) <= 1]
        return (near[0], near[-1] + 1) if near else (0, 0)

    def tile_of(ref, slot, kind, t):
        return ref[slot, t // 2, kind, (t % 2) * TILE:(t % 2 + 1) * TILE]

    def queries_of(t):
        return max(0, t - 1), min(SPAN, t + 2)

    def near_queries(tiles):
        return [c for c in range(SPAN) if keys_of(c, tiles)[1]]

    def place(slot):
        frame = chosen(slot, (0, 1, 2, 0, 0, 1, 1, 2, 2))
        frame = jnp.where(frame == 0, a, jnp.where(frame == 1, partner, cross))
        row = b + chosen(slot, (0, 0, 0, -1, 1, -1, 1, -1, 1))
        return frame, row

    def exists(slot):
        far = chosen(slot, (0, 0, 1, 0, 0, 0, 0, 1, 1))
        row = b + chosen(slot, (0, 0, 0, -1, 1, -1, 1, -1, 1))
        near = both(row >= 0, row < NH)
        return both(near, jnp.logical_or(far == 0, inner))

    def forward_unit(slot, tiles):
        frame, row = place(slot)
        for t in tiles:
            rows = slice(t * TILE, (t + 1) * TILE)
            kt_s[slot, :, rows] = tile_of(kv_s, slot, 0, t).T
            vt_s[slot, :, rows] = tile_of(kv_s, slot, 1, t).T
            valid = tv_s[frame, row, t:t + 1, :]
            bias = jnp.where(valid > 0, 0.0, LOWEST)
            mask_s[rows] = jnp.broadcast_to(bias, (HD, TILE)).T.astype(BF16)
        shrink = {}
        for c in near_queries(tiles):
            lo, hi = keys_of(c, tiles)
            keys = jnp.concatenate([tile_of(kv_s, slot, 0, t) for t in range(lo, hi)], axis=0)
            keys = jnp.concatenate([keys, mask_s[lo * TILE:hi * TILE]], axis=1)
            scores = dot(keys, qt_s[c])
            old = m_s[c]
            new = jnp.maximum(old, jnp.max(scores, axis=0, keepdims=True))
            weights = jnp.exp2((scores - new) * EXPO).astype(BF16)
            for t in range(lo, hi):
                p_s[slot, PAIR_AT[t, c]] = weights[(t - lo) * TILE:(t - lo + 1) * TILE]
            shrink[c] = jnp.exp2((old - new) * EXPO)
            m_s[c] = new
            for part in sorted({t // 2 for t in range(lo, hi)}):
                mb_s[slot, part, c] = new
        for c in near_queries(tiles):
            lo, hi = keys_of(c, tiles)
            rows = slice(lo * TILE, hi * TILE)
            vals = jnp.concatenate([vt_s[slot, :, rows], ones_rows[:, rows]], axis=0)
            weights = jnp.concatenate([p_s[slot, PAIR_AT[t, c]] for t in range(lo, hi)], axis=0)
            att_s[c] = att_s[c] * shrink[c] + dot(vals, weights)

    def grad_attended():
        for load in loads[2:]:
            load.wait()
        for n in range(0, D, HD):
            og_s[n:n + HD] = raw_s[n:n + HD].reshape(HD, TOKENS)
        for c in range(SPAN):
            rows = slice(c * TILE, (c + 1) * TILE)
            grad = dot(w_s[...], og_s[:, rows], ((0,), (0,))).astype(BF16)
            dot_s[c, :HD] = grad
            do_s[rows] = grad.T

    every = tuple(range(SPAN))

    def forward_pass(first, count, tiles, events):
        def step(i, carry):
            for at, waits in events.items():
                @pl.when(i == at - first)
                def _():
                    if at == 1:
                        grad_attended()
                    for source, part, starts in waits:
                        wait_unit(source, part)
                        for n in starts:
                            start_hop(n, part)

            @pl.when(exists(i + first))
            def _():
                forward_unit(i + first, tiles)

            return carry

        lax.fori_loop(0, count, step, 0)

    forward_pass(0, 2, every, {1: [(1, 0, ()), (1, 1, ())]})
    forward_pass(2, 5, (0, 1), {
        2: [(2, 0, ())],
        3: [(3, 0, (4, 8)), (4, 0, (5, 9))],
        5: [(2, 1, (6, 7)), (5, 0, ())],
        6: [(6, 0, ())],
    })
    forward_pass(2, 5, (2, 3), {3: [(3, 1, (4,)), (4, 1, (5,))], 5: [(5, 1, ())], 6: [(6, 1, ())]})
    forward_pass(7, 2, every, {7: [(7, 0, ()), (7, 1, ())], 8: [(8, 0, ()), (8, 1, ())]})

    for c in range(SPAN):
        rows = slice(c * TILE, (c + 1) * TILE)
        inverse = 1.0 / att_s[c, HD:HD + 1]
        rl_s[c] = inverse
        attended = (att_s[c, :HD] * inverse).astype(BF16)
        ag_s[h, :, rows] = attended
        delta = jnp.sum(dot_s[c, :HD].astype(F32) * attended.astype(F32), axis=0, keepdims=True)
        high = delta.astype(BF16).astype(F32)
        middle = (delta - high).astype(BF16).astype(F32)
        low = delta - high - middle
        index = lax.broadcasted_iota(jnp.int32, (HD, TILE), 0)
        extra = jnp.where(index == 0, -high, jnp.where(index == 1, -middle, jnp.where(index == 2, -low, 0.0)))
        dot_s[c, HD:] = extra.astype(BF16)
        dqt_s[c] = jnp.zeros((HD, TILE), F32)

    side = h + 1 - 2 * (h % 2)
    up, down = (h + 2) % HEADS, (h + HEADS - 2) % HEADS
    side_up, side_down = (side + 2) % HEADS, (side + HEADS - 2) % HEADS
    half = HD // 2
    low_half, high_half = pl.ds(0, half), pl.ds(half, half)
    gathers = [
        (ag_s.at[h], side),
        (ag_s.at[h], up),
        (ag_s.at[h], down),
        (ag_s.at[side], up),
        (ag_s.at[side], down),
        (ag_s.at[down, low_half], up),
        (ag_s.at[up, high_half], down),
        (ag_s.at[side_down, low_half], up),
        (ag_s.at[side_up, high_half], down),
    ]

    def gather_copy(n):
        block, peer = gathers[n]
        return remote(block, block, ag_send.at[n], ag_recv.at[n], (a, b, peer))

    def relay(waits, starts):
        for n in waits:
            gather_copy(n).wait_recv()
        for n in starts:
            gather_copy(n).start()

    relay((), (0, 1, 2))

    piece = D // GROUP
    chips = GROUP // 2
    chip = (a // 2) * NH + b

    def pair_copy():
        return remote(prod_s.at[1 - core], pair_s, pr_send.at[0], pr_recv.at[0], dev_partner)

    def part_copy(j):
        peer = (chip + j) % chips
        return remote(
            sum_s.at[peer], red_s.at[chip], pr_send.at[1], pr_recv.at[1], ((peer // NH) * 2 + core, peer % NH, h)
        )

    def part_copies():
        others = red_s.at[pl.ds(0, chips - 1)]
        return remote(others, others, pr_send.at[1], pr_recv.at[1], dev_partner)

    def weight_product():
        for of in (1 - core, core):
            for pair in range(NT // 2):
                first = pl.multiple_of((2 * pair + of) * NH * piece, NH * piece)
                value = dot(og_s[pl.ds(first, NH * piece)], ag_s[h], ((1,), (1,))).astype(BF16)
                for row in range(NH):
                    prod_s[of, pair * NH + row] = value[row * piece:(row + 1) * piece]
            if of is not core:
                pair_copy().start()

    def weight_parts():
        pair_copy().wait_recv()
        sum_s[...] = (prod_s[core].astype(F32) + pair_s[...].astype(F32)).astype(BF16)
        for j in range(1, chips):
            part_copy(j).start()

    for n in range(len(hops)):
        @pl.when(hops[n][3])
        def _():
            for part in hops[n][4]:
                hop_copy(n, part).wait_send()

    weight_product()

    @pl.when(inner)
    def _():
        weight_parts()

    def backward_unit(slot, tiles):
        factors = {
            (part, c): jnp.exp2((mb_s[slot, part, c] - m_s[c]) * EXPO) * rl_s[c]
            for part in sorted({t // 2 for t in tiles}) for c in near_queries((2 * part, 2 * part + 1))
        }
        for t in tiles:
            vals = jnp.concatenate([tile_of(kv_s, slot, 1, t), ones_cols], axis=1)
            for c in range(*queries_of(t)):
                n = PAIR_AT[t, c]
                grad = dot(vals, dot_s[c])
                probs = p_s[slot, n].astype(F32) * factors[t // 2, c]
                ps_s[n] = probs.astype(BF16)
                ds_s[n] = (probs * grad).astype(BF16)
        for t in tiles:
            rows = slice((t % 2) * TILE, (t % 2 + 1) * TILE)
            lo, hi = queries_of(t)
            near = slice(lo * TILE, hi * TILE)
            many_ds = jnp.concatenate([ds_s[PAIR_AT[t, c]] for c in range(lo, hi)], axis=1)
            many_ps = jnp.concatenate([ps_s[PAIR_AT[t, c]] for c in range(lo, hi)], axis=1)
            send_s[slot, t // 2, 0, rows] = (dot(many_ds, q_s[near]) * SCALE).astype(BF16)
            send_s[slot, t // 2, 1, rows] = dot(many_ps, do_s[near]).astype(BF16)
        for c in near_queries(tiles):
            lo, hi = keys_of(c, tiles)
            many = jnp.concatenate([ds_s[PAIR_AT[t, c]] for t in range(lo, hi)], axis=0)
            dqt_s[c] += dot(kt_s[slot, :, lo * TILE:hi * TILE], many)

    back = {
        (7, 0): (rd_s.at[0], 0, dev_cross, both(inner, has_lo), both(inner, has_lo)),
        (8, 0): (rd_s.at[1], 1, dev_cross, both(inner, has_hi), both(inner, has_hi)),
        (7, 1): (rx_s.at[0], 2, dev_lo, both(inner, has_lo), both(inner, has_hi)),
        (8, 1): (rx_s.at[1], 3, dev_hi, both(inner, has_hi), both(inner, has_lo)),
        (7, 2): (rw_s.at[0], 16, dev_lo, both(inner, has_lo), both(inner, has_hi)),
        (8, 2): (rw_s.at[1], 17, dev_hi, both(inner, has_hi), both(inner, has_lo)),
    }
    inside = {0: (0, 0), 2: (0, 1)}

    for part in range(2):
        at = 4 + 6 * part
        back[5, part] = (rp_s.at[1, part], at, dev_partner, has_lo, has_lo)
        back[6, part] = (rp_s.at[2, part], at + 1, dev_partner, has_hi, has_hi)
        back[3, part] = (rz_s.at[0, part], at + 2, dev_lo, has_lo, has_hi)
        back[4, part] = (rz_s.at[1, part], at + 3, dev_hi, has_hi, has_lo)
        back[2, part] = (ry_s.at[part], at + 4, dev_cross, inner, inner)
        back[1, part] = (rp_s.at[0, part], at + 5, dev_partner, yes, yes)
    needs = {key: () for key in back}
    needs[3, 0], needs[4, 0] = ((5, 0), (7, 0)), ((6, 0), (8, 0))
    needs[3, 1], needs[4, 1] = ((5, 1),), ((6, 1),)
    needs[2, 0] = ((7, 2), (8, 2))
    needs[2, 1] = ((7, 1), (8, 1))

    def back_copy(key):
        slot, part = key
        target, index, device, _, _ = back[key]
        source = send_s.at[(slot,) + inside[part]] if slot > 6 and part in inside else send_s.at[slot, part]
        return remote(source, target, f_send.at[index // 2, index % 2], b_recv.at[index], device)

    def merge(key, source):
        @pl.when(back[source][4])
        def _():
            back_copy(source).wait_recv()
            at = (key[0],) + inside[source[1]] if source[0] > 6 and source[1] in inside else key
            arrived = back[source][0][...].astype(F32)
            send_s[at] = (send_s[at].astype(F32) + arrived).astype(BF16)

    def give_back(key, who):
        @pl.when(both(who, back[key][3]))
        def _():
            for source in needs[key]:
                merge(key, source)
            back_copy(key).start()

    def first_step(i, carry):
        slot = jnp.where(inner, 7 + i, 3 + i)

        @pl.when(both(i == 1, outer))
        def _():
            weight_parts()

        @pl.when(exists(slot))
        def _():
            backward_unit(slot, every)

        for n in (7, 8):
            @pl.when(i == n - 7)
            def _():
                for part in range(3):
                    give_back((n, part), inner)

        return carry

    lax.fori_loop(0, 2, first_step, 0)

    @pl.when(outer)
    def _():
        relay((0,), (3, 4))

    for part in range(2):
        def partner_step(i, carry):
            if part == 1:
                @pl.when(both(i == 1, inner))
                def _():
                    relay((0,), (3, 4))

            @pl.when(exists(i + 5))
            def _():
                backward_unit(i + 5, (2 * part, 2 * part + 1))

            for n in (5, 6):
                @pl.when(i == n - 5)
                def _():
                    give_back((n, part), yes)

            return carry

        lax.fori_loop(0, 2, partner_step, 0)
        for n in (3, 4):
            give_back((n, part), outer)
        if part == 0:
            @pl.when(outer)
            def _():
                relay((1, 2), (5, 6))

    def last_step(i, carry):
        slot = chosen(i, LAST_ORDER)
        own_side = both(slot >= 3, outer)

        @pl.when(both(i == 0, inner))
        def _():
            relay((1, 2), (5, 6))

        @pl.when(i == 3)
        def _():
            wgat_s[core, h] = w_s[weight_rows(h)]
            weight_copies().wait_recv()
            weight_exchange().start()

        @pl.when(i == 4)
        def _():
            relay((3, 4), (7, 8))

        @pl.when(both(exists(slot), jnp.logical_not(own_side)))
        def _():
            backward_unit(slot, every)

        for n in range(1, 5):
            @pl.when(slot == n)
            def _():
                for part in range(2):
                    give_back((n, part), inner if n in (3, 4) else yes)

        return carry

    lax.fori_loop(0, len(LAST_ORDER), last_step, 0)

    for c in range(SPAN):
        rows = slice(c * TILE, (c + 1) * TILE)
        dq_s[rows] = (dqt_s[c] * SCALE).T.astype(BF16)

    stores = [
        pltpu.make_async_copy(src, dst, loc_sem.at[i])
        for i, (src, dst) in enumerate(
            [(mixed_s, mixed_ref), (dq_s, dq_ref), (dk_s, dk_ref), (dv_s, dv_ref), (wg_s, wg_ref)]
        )
    ]
    stores[1].start()

    def projected(heads):
        rows = [jnp.concatenate([wgat_s[i, n] for n in heads], axis=1) for i in range(2)]
        return dot(jnp.concatenate(rows, axis=0), jnp.concatenate([ag_s[n] for n in heads], axis=0))

    weight_exchange().wait_recv()
    most_s[...] = projected((h, side, up, down, side_up, side_down))
    for part in range(2):
        back_copy((1, part)).wait_recv()
        acc_s[part] = send_s[0, part].astype(F32) + rp_s[0, part].astype(F32)
    relay((5, 6, 7, 8), ())
    far = (h + HEADS // 2) % HEADS
    mixed = most_s[...] + projected((far, (side + HEADS // 2) % HEADS))
    mixed_s[...] = mixed.astype(BF16).reshape(share, SPAN, TILE)
    stores[0].start()

    for part in range(2):
        for source in (4, 3, 2):
            @pl.when(back[source, part][4])
            def _():
                back_copy((source, part)).wait_recv()
                acc_s[part] += back[source, part][0][...].astype(F32)
        rows = slice(part * HALF, (part + 1) * HALF)
        dk_s[rows] = acc_s[part, 0].astype(BF16)
        dv_s[rows] = acc_s[part, 1].astype(BF16)

    stores[2].start()
    stores[3].start()

    red_s[chip] = sum_s[chip]
    part_copies().wait_recv()
    total = red_s[0].astype(F32)
    for n in range(1, chips):
        total = total + red_s[n].astype(F32)
    wg_s[...] = total
    stores[4].start()

    for key, (_, _, _, sends, _) in back.items():
        @pl.when(sends)
        def _():
            back_copy(key).wait_send()
    weight_exchange().wait_send()
    weight_copies().wait_send()
    for n in range(len(gathers)):
        gather_copy(n).wait_send()
    pair_copy().wait_send()
    part_copies().wait_send()
    for store in stores:
        store.wait()


def hand_over(*refs):
    sources, targets, staged, sem = refs[:5], refs[5:10], refs[10:15], refs[15]
    reads = [pltpu.make_async_copy(sources[i], staged[i], sem.at[i]) for i in range(5)]
    writes = [pltpu.make_async_copy(staged[i], targets[i], sem.at[i]) for i in range(5)]
    for read in reads:
        read.start()
    for read, write in zip(reads, writes):
        read.wait()
        write.start()
    for write in writes:
        write.wait()


def per_device(queries, key_tiles, values, token_valid, out_weight, out_grad):
    any_spec = pl.BlockSpec(memory_space=pl.ANY)
    vmem = pltpu.VMEM
    dma = pltpu.SemaphoreType.DMA
    token = jax.ShapeDtypeStruct((TOKENS, HD), BF16)
    unit = (2, HALF, HD)
    pieces = (GROUP // 2, D // GROUP, HD)
    results = pl.pallas_call(
        kernel,
        out_shape=(
            jax.ShapeDtypeStruct((D // HEADS, SPAN, TILE), BF16),
            token, token, token,
            jax.ShapeDtypeStruct((D // GROUP, HD), F32),
        ),
        in_specs=[any_spec] * 6,
        out_specs=(any_spec,) * 5,
        scratch_shapes=[
            vmem((D // HEADS, SPAN, TILE), BF16),
            vmem((D // HEADS, TOKENS), F32),
            vmem((TOKENS, HD), BF16),
            vmem((TOKENS, HD), BF16),
            vmem((TOKENS, HD), BF16),
            vmem((D // GROUP, HD), F32),
            vmem((NT, NH, SPAN, TILE), jnp.int32),
            vmem((TOKENS, HD), BF16),
            vmem((SLOTS, 2) + unit, BF16),
            vmem((SLOTS, HD, TOKENS), BF16),
            vmem((SLOTS, HD, TOKENS), BF16),
            vmem((TOKENS, HD), BF16),
            vmem((D, HD), BF16),
            vmem((D, SPAN, TILE), BF16),
            vmem((D, TOKENS), BF16),
            vmem((SPAN, 2 * HD, TILE), BF16),
            vmem((TOKENS, HD), BF16),
            vmem((SPAN, 2 * HD, TILE), BF16),
            vmem((SLOTS, len(PAIRS), TILE, TILE), BF16),
            vmem((len(PAIRS), TILE, TILE), BF16),
            vmem((len(PAIRS), TILE, TILE), BF16),
            vmem((SPAN, HD + 16, TILE), F32),
            vmem((SPAN, 1, TILE), F32),
            vmem((SLOTS, 2, SPAN, 1, TILE), F32),
            vmem((SPAN, 1, TILE), F32),
            vmem((SPAN, HD, TILE), F32),
            vmem((2,) + unit, F32),
            vmem((SLOTS, 2) + unit, BF16),
            vmem((3, 2) + unit, BF16),
            vmem((2, 2) + unit, BF16),
            vmem((2,) + unit, BF16),
            vmem((2, HALF, HD), BF16),
            vmem((2, HALF, HD), BF16),
            vmem((2,) + unit, BF16),
            vmem((HEADS, HD, TOKENS), BF16),
            vmem((2, HEADS, D // HEADS // 2, HD), BF16),
            vmem((2,) + pieces, BF16),
            vmem(pieces, BF16),
            vmem(pieces, BF16),
            vmem(pieces, BF16),
            dma((5,)), dma((10, 2)), dma((SLOTS, 2)), dma((18,)),
            dma((9,)), dma((9,)), dma((2,)), dma((2,)), dma((2,)), dma((2,)),
        ],
        compiler_params=pltpu.CompilerParams(
            collective_id=0, has_side_effects=True, vmem_limit_bytes=60 * 1024 * 1024
        ),
    )(
        queries.reshape(TOKENS, HD),
        key_tiles.reshape(TOKENS, HD),
        values.reshape(TOKENS, HD),
        token_valid,
        out_weight,
        out_grad.reshape(D, SPAN, TILE),
    )
    mixed, dq, dk, dv, wg = pl.pallas_call(
        hand_over,
        out_shape=[jax.ShapeDtypeStruct(r.shape, r.dtype) for r in results],
        in_specs=[any_spec] * 5,
        out_specs=[any_spec] * 5,
        scratch_shapes=[vmem(r.shape, r.dtype) for r in results] + [dma((5,))],
    )(*results)
    tile_shape = (1, 1, 1, SPAN, TILE, HD)
    return (
        mixed.reshape(D // HEADS, 1, 1, SPAN, TILE),
        dq.reshape(tile_shape),
        dk.reshape(tile_shape),
        dv.reshape(tile_shape),
        wg,
    )


def solution(mesh):
    placed = (
        P("head", "tm", "height", None, None, None),
        P("head", "tm", "height", None, None, None),
        P("head", "tm", "height", None, None, None),
        P(),
        P(None, "head"),
        P(None, "tm", "height", None, None),
    )
    return jax.shard_map(
        per_device,
        mesh=mesh,
        in_specs=placed,
        out_specs=(
            P("head", "tm", "height", None, None),
            P("head", "tm", "height", None, None, None),
            P("head", "tm", "height", None, None, None),
            P("head", "tm", "height", None, None, None),
            P(("tm", "height"), "head"),
        ),
        check_vma=False,
    )
```

```python
import functools
import math

import jax
import jax.numpy as jnp
from jax import lax
from jax.experimental import pallas as pl
from jax.experimental.pallas import tpu as pltpu
from jax.sharding import PartitionSpec as P

MESH = pl.DeviceIdType.MESH
F32 = jnp.float32
BF16 = jnp.bfloat16

TILE = 256
SPAN = 4
TOKENS = TILE * SPAN
HD = 128
D = 1536
HEADS = 8
NT = 4
NH = 4
GROUP = NT * NH
SCALE = 1.0 / math.sqrt(HD)
EXPO = SCALE * math.log2(math.e)
LOWEST = -1e30

SLOTS = 9
HALF = TOKENS // 2
LAST_ORDER = (3, 2, 4, 1, 0)

PAIRS = [(k, q) for k in range(SPAN) for q in range(SPAN) if abs(k - q) <= 1]
PAIR_AT = {pair: i for i, pair in enumerate(PAIRS)}


def dot(lhs, rhs, dims=((1,), (0,))):
    return lax.dot_general(lhs, rhs, (dims, ((), ())), preferred_element_type=F32)


def chosen(index, table):
    value = jnp.int32(table[0])
    for at, entry in enumerate(table):
        value = jnp.where(index == at, jnp.int32(entry), value)
    return value


def kernel(
    q_ref, k_ref, v_ref, tv_ref, w_ref, og_ref,
    mixed_ref, dq_ref, dk_ref, dv_ref, wg_ref,
    mixed_s, most_s, dq_s, dk_s, dv_s, wg_s, tv_s,
    q_s, kv_s, kt_s, vt_s, mask_s, w_s, raw_s, og_s,
    qt_s, do_s, dot_s, p_s, ps_s, ds_s, att_s, m_s, mb_s, rl_s, dqt_s,
    acc_s, send_s, rp_s, rz_s, rx_s, rd_s, rw_s, ry_s, ag_s, wgat_s, prod_s, pair_s, sum_s, red_s,
    loc_sem, f_send, f_recv, b_recv, ag_send, ag_recv, wt_send, wt_recv, pr_send, pr_recv,
):
    a = lax.axis_index("tm")
    b = lax.axis_index("height")
    h = lax.axis_index("head")
    inner = jnp.logical_or(a == 1, a == 2)
    outer = jnp.logical_not(inner)
    has_lo = b > 0
    has_hi = b < NH - 1
    partner = a + 1 - 2 * (a % 2)
    cross = NT - 1 - a
    here = a * NH + b
    dev_partner = (partner, b, h)
    dev_cross = (cross, b, h)
    dev_lo = (a, b - 1, h)
    dev_hi = (a, b + 1, h)
    both = jnp.logical_and

    loads = [
        pltpu.make_async_copy(src, dst, loc_sem.at[i])
        for i, (src, dst) in enumerate([(q_ref, q_s), (tv_ref, tv_s), (w_ref, w_s), (og_ref, raw_s)])
    ]
    for part in range(2):
        for kind, ref in enumerate((k_ref, v_ref)):
            pltpu.make_async_copy(
                ref.at[pl.ds(part * HALF, HALF)], kv_s.at[0, part, kind], loc_sem.at[4]
            ).start()
    for load in loads:
        load.start()

    barrier = pltpu.get_barrier_semaphore()
    for j in range(1, GROUP):
        peer = (here + j) % GROUP
        pl.semaphore_signal(barrier, inc=1, device_id=(peer // NH, peer % NH, h), device_id_type=MESH)
    for j in range(1, HEADS):
        pl.semaphore_signal(barrier, inc=1, device_id=(a, b, (h + j) % HEADS), device_id_type=MESH)
    pl.semaphore_wait(barrier, GROUP - 1 + HEADS - 1)

    def remote(src, dst, send, recv, device):
        return pltpu.make_async_remote_copy(
            src_ref=src, dst_ref=dst, send_sem=send, recv_sem=recv, device_id=device, device_id_type=MESH
        )

    yes = a >= 0
    hops = [
        (0, 3, dev_hi, has_hi, (0, 1)),
        (0, 4, dev_lo, has_lo, (0, 1)),
        (0, 2, dev_cross, inner, (0, 1)),
        (0, 1, dev_partner, yes, (0, 1)),
        (3, 5, dev_partner, has_lo, (0, 1)),
        (4, 6, dev_partner, has_hi, (0, 1)),
        (2, 7, dev_hi, both(inner, has_hi), (1,)),
        (2, 8, dev_lo, both(inner, has_lo), (1,)),
        (3, 7, dev_cross, both(inner, has_lo), (0,)),
        (4, 8, dev_cross, both(inner, has_hi), (0,)),
    ]
    arrives = [yes, yes, inner, has_lo, has_hi, has_lo, has_hi, both(inner, has_lo), both(inner, has_hi)]

    def hop_copy(n, part):
        source, target, device, _, _ = hops[n]
        return remote(
            kv_s.at[source, part], kv_s.at[target, part], f_send.at[n, part], f_recv.at[target, part], device
        )

    def start_hop(n, part):
        @pl.when(hops[n][3])
        def _():
            hop_copy(n, part).start()

    def wait_unit(slot, part):
        @pl.when(arrives[slot])
        def _():
            remote(
                kv_s.at[slot, part], kv_s.at[slot, part], f_send.at[0, 0], f_recv.at[slot, part], dev_partner
            ).wait_recv()

    for part in range(2):
        for n in range(4):
            @pl.when(hops[n][3])
            def _():
                _, target, device, _, _ = hops[n]
                for kind, ref in enumerate((k_ref, v_ref)):
                    remote(
                        ref.at[pl.ds(part * HALF, HALF)], kv_s.at[target, part, kind],
                        f_send.at[n, part], f_recv.at[target, part], device,
                    ).start()

    share = D // HEADS

    part_share = share // 2
    core = a % 2

    def weight_rows(peer):
        return pl.ds(pl.multiple_of(peer * share + core * part_share, part_share), part_share)

    def weight_copy(j):
        peer = (h + j) % HEADS
        return remote(
            w_ref.at[weight_rows(peer)], wgat_s.at[core, h], wt_send.at[0], wt_recv.at[0], (a, b, peer)
        )

    def weight_exchange():
        return remote(wgat_s.at[core], wgat_s.at[core], wt_send.at[1], wt_recv.at[1], dev_partner)

    def weight_copies():
        others = wgat_s.at[core, pl.ds(0, HEADS - 1)]
        return remote(others, others, wt_send.at[0], wt_recv.at[0], dev_partner)

    for j in range(1, HEADS):
        weight_copy(j).start()

    loads[0].wait()
    loads[1].wait()
    pltpu.make_async_copy(kv_s.at[0], kv_s.at[0], loc_sem.at[4]).wait()
    first_row = (lax.broadcasted_iota(jnp.int32, (HD, TILE), 0) == 0).astype(BF16)
    for c in range(SPAN):
        rows = slice(c * TILE, (c + 1) * TILE)
        qt_s[c, :HD] = q_s[rows].T
        qt_s[c, HD:] = first_row
        m_s[c] = jnp.full((1, TILE), LOWEST, F32)
        att_s[c] = jnp.zeros((HD + 16, TILE), F32)
    ones_rows = jnp.ones((16, TOKENS), BF16)
    ones_cols = jnp.ones((TILE, HD), BF16)

    def keys_of(c, tiles):
        near = [t for t in tiles if abs(t - c) <= 1]
        return (near[0], near[-1] + 1) if near else (0, 0)

    def tile_of(ref, slot, kind, t):
        return ref[slot, t // 2, kind, (t % 2) * TILE:(t % 2 + 1) * TILE]

    def queries_of(t):
        return max(0, t - 1), min(SPAN, t + 2)

    def near_queries(tiles):
        return [c for c in range(SPAN) if keys_of(c, tiles)[1]]

    def place(slot):
        frame = chosen(slot, (0, 1, 2, 0, 0, 1, 1, 2, 2))
        frame = jnp.where(frame == 0, a, jnp.where(frame == 1, partner, cross))
        row = b + chosen(slot, (0, 0, 0, -1, 1, -1, 1, -1, 1))
        return frame, row

    def exists(slot):
        far = chosen(slot, (0, 0, 1, 0, 0, 0, 0, 1, 1))
        row = b + chosen(slot, (0, 0, 0, -1, 1, -1, 1, -1, 1))
        near = both(row >= 0, row < NH)
        return both(near, jnp.logical_or(far == 0, inner))

    def forward_unit(slot, tiles):
        frame, row = place(slot)
        for t in tiles:
            rows = slice(t * TILE, (t + 1) * TILE)
            kt_s[slot, :, rows] = tile_of(kv_s, slot, 0, t).T
            vt_s[slot, :, rows] = tile_of(kv_s, slot, 1, t).T
            valid = tv_s[frame, row, t:t + 1, :]
            bias = jnp.where(valid > 0, 0.0, LOWEST)
            mask_s[rows] = jnp.broadcast_to(bias, (HD, TILE)).T.astype(BF16)
        shrink = {}
        for c in near_queries(tiles):
            lo, hi = keys_of(c, tiles)
            keys = jnp.concatenate([tile_of(kv_s, slot, 0, t) for t in range(lo, hi)], axis=0)
            keys = jnp.concatenate([keys, mask_s[lo * TILE:hi * TILE]], axis=1)
            scores = dot(keys, qt_s[c])
            old = m_s[c]
            new = jnp.maximum(old, jnp.max(scores, axis=0, keepdims=True))
            weights = jnp.exp2((scores - new) * EXPO).astype(BF16)
            for t in range(lo, hi):
                p_s[slot, PAIR_AT[t, c]] = weights[(t - lo) * TILE:(t - lo + 1) * TILE]
            shrink[c] = jnp.exp2((old - new) * EXPO)
            m_s[c] = new
            for part in sorted({t // 2 for t in range(lo, hi)}):
                mb_s[slot, part, c] = new
        for c in near_queries(tiles):
            lo, hi = keys_of(c, tiles)
            rows = slice(lo * TILE, hi * TILE)
            vals = jnp.concatenate([vt_s[slot, :, rows], ones_rows[:, rows]], axis=0)
            weights = jnp.concatenate([p_s[slot, PAIR_AT[t, c]] for t in range(lo, hi)], axis=0)
            att_s[c] = att_s[c] * shrink[c] + dot(vals, weights)

    def grad_attended():
        for load in loads[2:]:
            load.wait()
        for n in range(0, D, HD):
            og_s[n:n + HD] = raw_s[n:n + HD].reshape(HD, TOKENS)
        for c in range(SPAN):
            rows = slice(c * TILE, (c + 1) * TILE)
            grad = dot(w_s[...], og_s[:, rows], ((0,), (0,))).astype(BF16)
            dot_s[c, :HD] = grad
            do_s[rows] = grad.T

    every = tuple(range(SPAN))

    def forward_pass(first, count, tiles, events):
        def step(i, carry):
            for at, waits in events.items():
                @pl.when(i == at - first)
                def _():
                    if at == 1:
                        grad_attended()
                    for source, part, starts in waits:
                        wait_unit(source, part)
                        for n in starts:
                            start_hop(n, part)

            @pl.when(exists(i + first))
            def _():
                forward_unit(i + first, tiles)

            return carry

        lax.fori_loop(0, count, step, 0)

    forward_pass(0, 2, every, {1: [(1, 0, ()), (1, 1, ())]})
    forward_pass(2, 5, (0, 1), {
        2: [(2, 0, ())],
        3: [(3, 0, (4, 8)), (4, 0, (5, 9))],
        5: [(2, 1, (6, 7)), (5, 0, ())],
        6: [(6, 0, ())],
    })
    forward_pass(2, 5, (2, 3), {3: [(3, 1, (4,)), (4, 1, (5,))], 5: [(5, 1, ())], 6: [(6, 1, ())]})
    forward_pass(7, 2, every, {7: [(7, 0, ()), (7, 1, ())], 8: [(8, 0, ()), (8, 1, ())]})

    for c in range(SPAN):
        rows = slice(c * TILE, (c + 1) * TILE)
        inverse = 1.0 / att_s[c, HD:HD + 1]
        rl_s[c] = inverse
        attended = (att_s[c, :HD] * inverse).astype(BF16)
        ag_s[h, :, rows] = attended
        delta = jnp.sum(dot_s[c, :HD].astype(F32) * attended.astype(F32), axis=0, keepdims=True)
        high = delta.astype(BF16).astype(F32)
        middle = (delta - high).astype(BF16).astype(F32)
        low = delta - high - middle
        index = lax.broadcasted_iota(jnp.int32, (HD, TILE), 0)
        extra = jnp.where(index == 0, -high, jnp.where(index == 1, -middle, jnp.where(index == 2, -low, 0.0)))
        dot_s[c, HD:] = extra.astype(BF16)
        dqt_s[c] = jnp.zeros((HD, TILE), F32)

    side = h + 1 - 2 * (h % 2)
    up, down = (h + 2) % HEADS, (h + HEADS - 2) % HEADS
    side_up, side_down = (side + 2) % HEADS, (side + HEADS - 2) % HEADS
    half = HD // 2
    low_half, high_half = pl.ds(0, half), pl.ds(half, half)
    gathers = [
        (ag_s.at[h], side),
        (ag_s.at[h], up),
        (ag_s.at[h], down),
        (ag_s.at[side], up),
        (ag_s.at[side], down),
        (ag_s.at[down, low_half], up),
        (ag_s.at[up, high_half], down),
        (ag_s.at[side_down, low_half], up),
        (ag_s.at[side_up, high_half], down),
    ]

    def gather_copy(n):
        block, peer = gathers[n]
        return remote(block, block, ag_send.at[n], ag_recv.at[n], (a, b, peer))

    def relay(waits, starts):
        for n in waits:
            gather_copy(n).wait_recv()
        for n in starts:
            gather_copy(n).start()

    relay((), (0, 1, 2))

    piece = D // GROUP
    chips = GROUP // 2
    chip = (a // 2) * NH + b

    def pair_copy():
        return remote(prod_s.at[1 - core], pair_s, pr_send.at[0], pr_recv.at[0], dev_partner)

    def part_copy(j):
        peer = (chip + j) % chips
        return remote(
            sum_s.at[peer], red_s.at[chip], pr_send.at[1], pr_recv.at[1], ((peer // NH) * 2 + core, peer % NH, h)
        )

    def part_copies():
        others = red_s.at[pl.ds(0, chips - 1)]
        return remote(others, others, pr_send.at[1], pr_recv.at[1], dev_partner)

    def weight_product():
        for of in (1 - core, core):
            for pair in range(NT // 2):
                first = pl.multiple_of((2 * pair + of) * NH * piece, NH * piece)
                value = dot(og_s[pl.ds(first, NH * piece)], ag_s[h], ((1,), (1,))).astype(BF16)
                for row in range(NH):
                    prod_s[of, pair * NH + row] = value[row * piece:(row + 1) * piece]
            if of is not core:
                pair_copy().start()

    def weight_parts():
        pair_copy().wait_recv()
        sum_s[...] = (prod_s[core].astype(F32) + pair_s[...].astype(F32)).astype(BF16)
        for j in range(1, chips):
            part_copy(j).start()

    for n in range(len(hops)):
        @pl.when(hops[n][3])
        def _():
            for part in hops[n][4]:
                hop_copy(n, part).wait_send()

    weight_product()

    @pl.when(inner)
    def _():
        weight_parts()

    def backward_unit(slot, tiles):
        factors = {
            (part, c): jnp.exp2((mb_s[slot, part, c] - m_s[c]) * EXPO) * rl_s[c]
            for part in sorted({t // 2 for t in tiles}) for c in near_queries((2 * part, 2 * part + 1))
        }
        for t in tiles:
            vals = jnp.concatenate([tile_of(kv_s, slot, 1, t), ones_cols], axis=1)
            for c in range(*queries_of(t)):
                n = PAIR_AT[t, c]
                grad = dot(vals, dot_s[c])
                probs = p_s[slot, n].astype(F32) * factors[t // 2, c]
                ps_s[n] = probs.astype(BF16)
                ds_s[n] = (probs * grad).astype(BF16)
        for t in tiles:
            rows = slice((t % 2) * TILE, (t % 2 + 1) * TILE)
            lo, hi = queries_of(t)
            near = slice(lo * TILE, hi * TILE)
            many_ds = jnp.concatenate([ds_s[PAIR_AT[t, c]] for c in range(lo, hi)], axis=1)
            many_ps = jnp.concatenate([ps_s[PAIR_AT[t, c]] for c in range(lo, hi)], axis=1)
            send_s[slot, t // 2, 0, rows] = (dot(many_ds, q_s[near]) * SCALE).astype(BF16)
            send_s[slot, t // 2, 1, rows] = dot(many_ps, do_s[near]).astype(BF16)
        for c in near_queries(tiles):
            lo, hi = keys_of(c, tiles)
            many = jnp.concatenate([ds_s[PAIR_AT[t, c]] for t in range(lo, hi)], axis=0)
            dqt_s[c] += dot(kt_s[slot, :, lo * TILE:hi * TILE], many)

    back = {
        (7, 0): (rd_s.at[0], 0, dev_cross, both(inner, has_lo), both(inner, has_lo)),
        (8, 0): (rd_s.at[1], 1, dev_cross, both(inner, has_hi), both(inner, has_hi)),
        (7, 1): (rx_s.at[0], 2, dev_lo, both(inner, has_lo), both(inner, has_hi)),
        (8, 1): (rx_s.at[1], 3, dev_hi, both(inner, has_hi), both(inner, has_lo)),
        (7, 2): (rw_s.at[0], 16, dev_lo, both(inner, has_lo), both(inner, has_hi)),
        (8, 2): (rw_s.at[1], 17, dev_hi, both(inner, has_hi), both(inner, has_lo)),
    }
    inside = {0: (0, 0), 2: (0, 1)}

    for part in range(2):
        at = 4 + 6 * part
        back[5, part] = (rp_s.at[1, part], at, dev_partner, has_lo, has_lo)
        back[6, part] = (rp_s.at[2, part], at + 1, dev_partner, has_hi, has_hi)
        back[3, part] = (rz_s.at[0, part], at + 2, dev_lo, has_lo, has_hi)
        back[4, part] = (rz_s.at[1, part], at + 3, dev_hi, has_hi, has_lo)
        back[2, part] = (ry_s.at[part], at + 4, dev_cross, inner, inner)
        back[1, part] = (rp_s.at[0, part], at + 5, dev_partner, yes, yes)
    needs = {key: () for key in back}
    needs[3, 0], needs[4, 0] = ((5, 0), (7, 0)), ((6, 0), (8, 0))
    needs[3, 1], needs[4, 1] = ((5, 1),), ((6, 1),)
    needs[2, 0] = ((7, 2), (8, 2))
    needs[2, 1] = ((7, 1), (8, 1))

    def back_copy(key):
        slot, part = key
        target, index, device, _, _ = back[key]
        source = send_s.at[(slot,) + inside[part]] if slot > 6 and part in inside else send_s.at[slot, part]
        return remote(source, target, f_send.at[index // 2, index % 2], b_recv.at[index], device)

    def merge(key, source):
        @pl.when(back[source][4])
        def _():
            back_copy(source).wait_recv()
            at = (key[0],) + inside[source[1]] if source[0] > 6 and source[1] in inside else key
            arrived = back[source][0][...].astype(F32)
            send_s[at] = (send_s[at].astype(F32) + arrived).astype(BF16)

    def give_back(key, who):
        @pl.when(both(who, back[key][3]))
        def _():
            for source in needs[key]:
                merge(key, source)
            back_copy(key).start()

    def first_step(i, carry):
        slot = jnp.where(inner, 7 + i, 3 + i)

        @pl.when(both(i == 1, outer))
        def _():
            weight_parts()

        @pl.when(exists(slot))
        def _():
            backward_unit(slot, every)

        for n in (7, 8):
            @pl.when(i == n - 7)
            def _():
                for part in range(3):
                    give_back((n, part), inner)

        return carry

    lax.fori_loop(0, 2, first_step, 0)

    @pl.when(outer)
    def _():
        relay((0,), (3, 4))

    for part in range(2):
        def partner_step(i, carry):
            if part == 1:
                @pl.when(both(i == 1, inner))
                def _():
                    relay((0,), (3, 4))

            @pl.when(exists(i + 5))
            def _():
                backward_unit(i + 5, (2 * part, 2 * part + 1))

            for n in (5, 6):
                @pl.when(i == n - 5)
                def _():
                    give_back((n, part), yes)

            return carry

        lax.fori_loop(0, 2, partner_step, 0)
        for n in (3, 4):
            give_back((n, part), outer)
        if part == 0:
            @pl.when(outer)
            def _():
                relay((1, 2), (5, 6))

    def last_step(i, carry):
        slot = chosen(i, LAST_ORDER)
        own_side = both(slot >= 3, outer)

        @pl.when(both(i == 0, inner))
        def _():
            relay((1, 2), (5, 6))

        @pl.when(i == 3)
        def _():
            wgat_s[core, h] = w_s[weight_rows(h)]
            weight_copies().wait_recv()
            weight_exchange().start()

        @pl.when(i == 4)
        def _():
            relay((3, 4), (7, 8))

        @pl.when(both(exists(slot), jnp.logical_not(own_side)))
        def _():
            backward_unit(slot, every)

        for n in range(1, 5):
            @pl.when(slot == n)
            def _():
                for part in range(2):
                    give_back((n, part), inner if n in (3, 4) else yes)

        return carry

    lax.fori_loop(0, len(LAST_ORDER), last_step, 0)

    for c in range(SPAN):
        rows = slice(c * TILE, (c + 1) * TILE)
        dq_s[rows] = (dqt_s[c] * SCALE).T.astype(BF16)

    stores = [
        pltpu.make_async_copy(src, dst, loc_sem.at[i])
        for i, (src, dst) in enumerate(
            [(mixed_s, mixed_ref), (dq_s, dq_ref), (dk_s, dk_ref), (dv_s, dv_ref), (wg_s, wg_ref)]
        )
    ]
    stores[1].start()

    def projected(heads):
        rows = [jnp.concatenate([wgat_s[i, n] for n in heads], axis=1) for i in range(2)]
        return dot(jnp.concatenate(rows, axis=0), jnp.concatenate([ag_s[n] for n in heads], axis=0))

    weight_exchange().wait_recv()
    most_s[...] = projected((h, side, up, down, side_up, side_down))
    for part in range(2):
        back_copy((1, part)).wait_recv()
        acc_s[part] = send_s[0, part].astype(F32) + rp_s[0, part].astype(F32)
    relay((5, 6, 7, 8), ())
    far = (h + HEADS // 2) % HEADS
    mixed = most_s[...] + projected((far, (side + HEADS // 2) % HEADS))
    mixed_s[...] = mixed.astype(BF16).reshape(share, SPAN, TILE)
    stores[0].start()

    for part in range(2):
        for source in (4, 3, 2):
            @pl.when(back[source, part][4])
            def _():
                back_copy((source, part)).wait_recv()
                acc_s[part] += back[source, part][0][...].astype(F32)
        rows = slice(part * HALF, (part + 1) * HALF)
        dk_s[rows] = acc_s[part, 0].astype(BF16)
        dv_s[rows] = acc_s[part, 1].astype(BF16)
        for kind, target in ((0, dk_ref), (1, dv_ref)):
            pltpu.make_async_copy((dk_s, dv_s)[kind].at[rows], target.at[rows], loc_sem.at[2 + kind]).start()


    red_s[chip] = sum_s[chip]
    part_copies().wait_recv()
    total = red_s[0].astype(F32)
    for n in range(1, chips):
        total = total + red_s[n].astype(F32)
    wg_s[...] = total
    stores[4].start()

    for key, (_, _, _, sends, _) in back.items():
        @pl.when(sends)
        def _():
            back_copy(key).wait_send()
    weight_exchange().wait_send()
    weight_copies().wait_send()
    for n in range(len(gathers)):
        gather_copy(n).wait_send()
    pair_copy().wait_send()
    part_copies().wait_send()
    for store in stores:
        store.wait()


def hand_over(*refs):
    sources, targets, staged, sem = refs[:5], refs[5:10], refs[10:15], refs[15]
    reads = [pltpu.make_async_copy(sources[i], staged[i], sem.at[i]) for i in range(5)]
    writes = [pltpu.make_async_copy(staged[i], targets[i], sem.at[i]) for i in range(5)]
    for read in reads:
        read.start()
    for read, write in zip(reads, writes):
        read.wait()
        write.start()
    for write in writes:
        write.wait()


def per_device(queries, key_tiles, values, token_valid, out_weight, out_grad):
    any_spec = pl.BlockSpec(memory_space=pl.ANY)
    vmem = pltpu.VMEM
    dma = pltpu.SemaphoreType.DMA
    token = jax.ShapeDtypeStruct((TOKENS, HD), BF16)
    unit = (2, HALF, HD)
    pieces = (GROUP // 2, D // GROUP, HD)
    results = pl.pallas_call(
        kernel,
        out_shape=(
            jax.ShapeDtypeStruct((D // HEADS, SPAN, TILE), BF16),
            token, token, token,
            jax.ShapeDtypeStruct((D // GROUP, HD), F32),
        ),
        in_specs=[any_spec] * 6,
        out_specs=(any_spec,) * 5,
        scratch_shapes=[
            vmem((D // HEADS, SPAN, TILE), BF16),
            vmem((D // HEADS, TOKENS), F32),
            vmem((TOKENS, HD), BF16),
            vmem((TOKENS, HD), BF16),
            vmem((TOKENS, HD), BF16),
            vmem((D // GROUP, HD), F32),
            vmem((NT, NH, SPAN, TILE), jnp.int32),
            vmem((TOKENS, HD), BF16),
            vmem((SLOTS, 2) + unit, BF16),
            vmem((SLOTS, HD, TOKENS), BF16),
            vmem((SLOTS, HD, TOKENS), BF16),
            vmem((TOKENS, HD), BF16),
            vmem((D, HD), BF16),
            vmem((D, SPAN, TILE), BF16),
            vmem((D, TOKENS), BF16),
            vmem((SPAN, 2 * HD, TILE), BF16),
            vmem((TOKENS, HD), BF16),
            vmem((SPAN, 2 * HD, TILE), BF16),
            vmem((SLOTS, len(PAIRS), TILE, TILE), BF16),
            vmem((len(PAIRS), TILE, TILE), BF16),
            vmem((len(PAIRS), TILE, TILE), BF16),
            vmem((SPAN, HD + 16, TILE), F32),
            vmem((SPAN, 1, TILE), F32),
            vmem((SLOTS, 2, SPAN, 1, TILE), F32),
            vmem((SPAN, 1, TILE), F32),
            vmem((SPAN, HD, TILE), F32),
            vmem((2,) + unit, F32),
            vmem((SLOTS, 2) + unit, BF16),
            vmem((3, 2) + unit, BF16),
            vmem((2, 2) + unit, BF16),
            vmem((2,) + unit, BF16),
            vmem((2, HALF, HD), BF16),
            vmem((2, HALF, HD), BF16),
            vmem((2,) + unit, BF16),
            vmem((HEADS, HD, TOKENS), BF16),
            vmem((2, HEADS, D // HEADS // 2, HD), BF16),
            vmem((2,) + pieces, BF16),
            vmem(pieces, BF16),
            vmem(pieces, BF16),
            vmem(pieces, BF16),
            dma((5,)), dma((10, 2)), dma((SLOTS, 2)), dma((18,)),
            dma((9,)), dma((9,)), dma((2,)), dma((2,)), dma((2,)), dma((2,)),
        ],
        compiler_params=pltpu.CompilerParams(
            collective_id=0, has_side_effects=True, vmem_limit_bytes=60 * 1024 * 1024
        ),
    )(
        queries.reshape(TOKENS, HD),
        key_tiles.reshape(TOKENS, HD),
        values.reshape(TOKENS, HD),
        token_valid,
        out_weight,
        out_grad.reshape(D, SPAN, TILE),
    )
    mixed, dq, dk, dv, wg = pl.pallas_call(
        hand_over,
        out_shape=[jax.ShapeDtypeStruct(r.shape, r.dtype) for r in results],
        in_specs=[any_spec] * 5,
        out_specs=[any_spec] * 5,
        scratch_shapes=[vmem(r.shape, r.dtype) for r in results] + [dma((5,))],
    )(*results)
    tile_shape = (1, 1, 1, SPAN, TILE, HD)
    return (
        mixed.reshape(D // HEADS, 1, 1, SPAN, TILE),
        dq.reshape(tile_shape),
        dk.reshape(tile_shape),
        dv.reshape(tile_shape),
        wg,
    )


def solution(mesh):
    placed = (
        P("head", "tm", "height", None, None, None),
        P("head", "tm", "height", None, None, None),
        P("head", "tm", "height", None, None, None),
        P(),
        P(None, "head"),
        P(None, "tm", "height", None, None),
    )
    return jax.shard_map(
        per_device,
        mesh=mesh,
        in_specs=placed,
        out_specs=(
            P("head", "tm", "height", None, None),
            P("head", "tm", "height", None, None, None),
            P("head", "tm", "height", None, None, None),
            P("head", "tm", "height", None, None, None),
            P(("tm", "height"), "head"),
        ),
        check_vma=False,
    )
```
